128 devices in a mesh: face: 4 (over y), blk: 32 (over z, x, core).
Axes of the slice: x: 4, y: 4, z: 4, core: 2. Of those that a mesh axis runs over, the one named last changes fastest.
Arguments:
- field: bfloat16 [8192, 64, 128], P(('face', 'blk')), may hold values from -6 to 6
- patch_rows: int32 [384, 64], P(('face', 'blk')), may hold values from 0 to 8191, as said below
- flips: int32 [384, 64], P(('face', 'blk')), may hold values from 0 to 1, as said below
- blend_weights: int32 [384, 64, 64], P(('face', 'blk')), may hold values from 1 to 8
- live: int32 [128], P(('face', 'blk')), may hold values from 2 to 3, as said below
- kernel_one: bfloat16 [3, 3, 128, 128], replicated, may hold values from -0.1875 to 0.1875
- bias_one: float32 [128], replicated, may hold values from -3 to 3
- kernel_two: bfloat16 [3, 3, 128, 128], replicated, may hold values from -0.1875 to 0.1875
- bias_two: float32 [128], replicated, may hold values from -3 to 3
Outputs:
- blended: bfloat16 [8192, 64, 128], P(('face', 'blk'))
The draws below stay inside these ranges and needn't reach their ends.
Inputs may be any that keep to these rules, and one draw needn't show every extreme that they name: `patch_rows`: device d's slots list 64 consecutive rows modulo 8192 each, starting between d * 64 - 32 and (d + 1) * 64 - 32; reads reach exactly 32 rows beyond device 0's rows on both sides; every row is read by some live slot; slots that are not live hold valid rows and are ignored. `flips`: 1 exactly where the row lies in another face group than the slot's device. Device 0 has all 3 slots live.
All inputs are finite; a program needn't handle non-finite values.
Results may differ from the reference program's by a relative error of at most 0.006.
Values may be sent and summed in bfloat16 or wider, within the bound.
A program may use at most 192 MiB of HBM per device.

```python
import jax
import jax.numpy as jnp
from jax import lax

C = 128
PS = 64
RIM = 32
ROW_DEV = 64
PCAP = 3
NROW = 8192
FACE_ROWS = 2048
NPATCH = 384


def patch_layout(key):
    devices = NROW // ROW_DEV
    live = jax.random.randint(jax.random.fold_in(key, 101), (devices,), 2, PCAP + 1)
    live = live.at[devices - 1].set(2).at[0].set(PCAP)
    lower = jax.random.randint(jax.random.fold_in(key, 102), (devices,), 0, RIM + 1).at[0].set(0)
    upper = jax.random.randint(jax.random.fold_in(key, 103), (devices,), 0, RIM + 1).at[0].set(0)
    span = ROW_DEV + 2 * RIM - PS
    extra = jax.random.randint(jax.random.fold_in(key, 104), (devices, PCAP), 0, span + 1)
    lowest = jnp.arange(devices, dtype=jnp.int32) * ROW_DEV - RIM
    starts = lowest[:, None] + extra
    starts = starts.at[:, 0].set(lowest + lower).at[:, 1].set(lowest + span - upper)
    row_list = jnp.mod(starts.reshape(-1)[:, None] + jnp.arange(PS, dtype=jnp.int32)[None, :], NROW)
    return (live.astype(jnp.int32), row_list.astype(jnp.int32))


def draw_patch_rows(key, part):
    live, row_list = patch_layout(key)
    return row_list


def draw_flips(key, part):
    live, row_list = patch_layout(key)
    owner_face = jnp.arange(NPATCH, dtype=jnp.int32) // PCAP * ROW_DEV // FACE_ROWS
    source_face = row_list // FACE_ROWS
    return (source_face != owner_face[:, None]).astype(jnp.int32)


def draw_live(key, part):
    live, row_list = patch_layout(key)
    return live


def plant(array, own_key, low, high):
    place = [jax.random.randint(jax.random.fold_in(own_key, axis), (), 0, length) for axis, length in enumerate(array.shape)]
    main_axis = array.shape.index(max(array.shape))
    next_to = place[:main_axis] + [(place[main_axis] + 1) % array.shape[main_axis]] + place[main_axis + 1:]
    return array.at[tuple(place)].set(low).at[tuple(next_to)].set(high)


def block_scale(rng, dims, cuts, least, largest):
    gain, own = 1.0, jax.random.fold_in(rng, 6)
    for dim, parts in cuts:
        draws = jnp.exp(jax.random.uniform(jax.random.fold_in(own, dim), (parts,), jnp.float32, least / len(cuts), largest / len(cuts)))
        gain = gain * jnp.repeat(draws, dims[dim] // parts).reshape([-1 if axis == dim else 1 for axis in range(len(dims))])
    return gain


def gaussian(stream_key, shape, deviation, limit, pieces=(), held_as=jnp.bfloat16):
    factor_of = block_scale(stream_key, shape, pieces, -0.22, 0.18) if pieces else 1.0
    drawn = jax.random.normal(stream_key, shape, jnp.float32) * deviation * factor_of
    return jnp.minimum(jnp.maximum(drawn, -limit), limit).astype(held_as)


def setup_inputs(seed: int = 0) -> dict:
    streams_of = jax.random.split(jax.random.key(seed), 10)
    return {
        "field": gaussian(streams_of[0], (NROW, PS, C), 1.0, 6.0, ((0, 128),)),
        "patch_rows": draw_patch_rows(jax.random.fold_in(streams_of[9], 71), 0),
        "flips": draw_flips(jax.random.fold_in(streams_of[9], 71), 0),
        "blend_weights": plant(jax.random.randint(streams_of[3], (NPATCH, PS, PS), 1, 9), jax.random.fold_in(streams_of[3], 1), 1, 8).astype(jnp.int32),
        "live": draw_live(jax.random.fold_in(streams_of[9], 71), 0),
        "kernel_one": gaussian(streams_of[5], (3, 3, C, C), (9 * C) ** -0.5, 0.1875),
        "bias_one": gaussian(streams_of[6], (C,), 0.5, 3.0, (), jnp.float32),
        "kernel_two": gaussian(streams_of[7], (3, 3, C, C), (9 * C) ** -0.5, 0.1875),
        "bias_two": gaussian(streams_of[8], (C,), 0.5, 3.0, (), jnp.float32),
    }


def conv_block(picture, kernel_one, bias_one, kernel_two, bias_two):
    numbers = ("NHWC", "HWIO", "NHWC")
    first_conv = lax.conv_general_dilated(picture[None], kernel_one, (1, 1), "SAME", dimension_numbers=numbers, preferred_element_type=jnp.float32)[0]
    hidden = jax.nn.silu(first_conv + bias_one).astype(jnp.bfloat16)
    second_conv = lax.conv_general_dilated(hidden[None], kernel_two, (1, 1), "SAME", dimension_numbers=numbers, preferred_element_type=jnp.float32)[0]
    return picture.astype(jnp.float32) + second_conv + bias_two


def reference(field, patch_rows, flips, blend_weights, live, kernel_one, bias_one, kernel_two, bias_two):
    summed = jnp.zeros(field.shape, jnp.float32)
    coverage = jnp.zeros(field.shape[:2], jnp.float32)

    def visit(current, number):
        owner_device = number // PCAP
        slot_number = number % PCAP

        def apply(state):
            summed, coverage = state
            row_list = patch_rows[number]
            turned = flips[number] == 1
            picture = jnp.take(field, row_list, axis=0)
            picture = jnp.where(turned[:, None, None], picture[:, ::-1], picture)
            result = conv_block(picture, kernel_one, bias_one, kernel_two, bias_two)
            weight = blend_weights[number].astype(jnp.float32)
            weighted = result * weight[:, :, None]
            returned = jnp.where(turned[:, None, None], weighted[:, ::-1], weighted)
            weight_back = jnp.where(turned[:, None], weight[:, ::-1], weight)
            return summed.at[row_list].add(returned), coverage.at[row_list].add(weight_back)

        def keep(unchanged):
            return unchanged

        return lax.cond(slot_number < live[owner_device], apply, keep, current), None

    (summed, coverage), _ = lax.scan(visit, (summed, coverage), jnp.arange(NPATCH, dtype=jnp.int32))
    return (summed / coverage[:, :, None]).astype(jnp.bfloat16)
```

```python
import functools

import jax
import jax.numpy as jnp
from jax import lax
from jax.experimental import pallas as pl
from jax.experimental.pallas import tpu as pltpu
from jax.sharding import PartitionSpec as P

MESH = pl.DeviceIdType.MESH
F32, BF16, I32 = jnp.float32, jnp.bfloat16, jnp.int32
SIDE, C, RIM, SLOTS = 64, 128, 32, 3
LINE = 8
X_ZERO = 68
H_ZERO = 66
H_EDGE = 67
N_EDGE = 12
N_ROWS = 18


def shifts(rows):
    column = lax.broadcasted_iota(I32, rows.shape, 1)
    left = jnp.where(column == 0, 0.0, pltpu.roll(rows, 1, 1))
    right = jnp.where(column == SIDE - 1, 0.0, pltpu.roll(rows, SIDE - 1, 1))
    return left, rows, right


def pair_rows(rows):
    n = rows.shape[0] // 2
    rows = rows.reshape(n, 2, SIDE, C)
    return jnp.concatenate([rows[:, 0], rows[:, 1]], axis=-1).reshape(n * SIDE, 2 * C)


def pair_dot(parts, w_ref, conv):
    lhs = jnp.concatenate([parts[t][p] for t in range(3) for p in range(2)], axis=-1)
    rhs = jnp.concatenate(
        [w_ref[conv, 2 * p : 2 * p + 2, t].reshape(2 * C, 2 * C) for t in range(3) for p in range(2)], axis=0
    )
    return jnp.dot(lhs, rhs, preferred_element_type=F32)


def unpair(wide):
    n = wide.shape[0] // SIDE
    return jnp.stack(
        [wide[:, :C].reshape(n, SIDE, C), wide[:, C:].reshape(n, SIDE, C)], axis=1
    )


def silu(z):
    return z * (0.5 + 0.5 * jnp.tanh(0.5 * z))


def work(
    faces, blks,
    field, rows, live, weights, k_one, k_two, b_one, b_two,
    base_out, edge_out, index_out,
    x3, h3, r_main, r_turn, wmat, wts, w_send, rim_in, w_in, rows_in, wown, wnear, cov, inside, base, edge, index,
    rows_s, live_s,
    field_sem, load_sem, send_sem, recv_sem, out_sem,
):
    me_face, me_blk = lax.axis_index("face"), lax.axis_index("blk")
    total = faces * blks
    me = me_face * blks + me_blk
    following = lax.rem(me + 1, total)
    preceding = lax.rem(me + total - 1, total)
    after = (following // blks, lax.rem(following, blks))
    before = (preceding // blks, lax.rem(preceding, blks))
    first = jnp.where(me_blk == 0, 1, 0)
    last = jnp.where(me_blk == blks - 1, 1, 0)
    boundary = jnp.logical_or(me_blk == 0, me_blk == blks - 1)
    n_total = total * SIDE

    barrier = pltpu.get_barrier_semaphore()
    for other in (after, before):
        pl.semaphore_signal(barrier, inc=1, device_id=other, device_id_type=MESH)

    small_loads = [
        pltpu.make_async_copy(live, live_s, load_sem.at[5]),
        pltpu.make_async_copy(rows, rows_s, load_sem.at[6]),
        pltpu.make_async_copy(weights, wts, load_sem.at[0]),
    ]
    for c in small_loads:
        c.start()
    field_loads = [
        pltpu.make_async_copy(field.at[pl.ds(16 * n, 16)], x3.at[1, pl.ds(2 + 16 * n, 16)], field_sem.at[n])
        for n in range(4)
    ]
    kernel_loads = [
        pltpu.make_async_copy(
            src, wmat.at[conv, pl.ds(q, 3), :, :, pl.ds(q * C, C)], load_sem.at[1 + 2 * conv + q]
        )
        for conv, src in enumerate((k_one, k_two)) for q in range(2)
    ]
    for c in field_loads[:2] + kernel_loads[:2] + field_loads[2:] + kernel_loads[2:]:
        c.start()

    for conv in range(2):
        wmat[conv, 0, :, :, C:] = jnp.zeros((3, C, C), BF16)
        wmat[conv, 3, :, :, :C] = jnp.zeros((3, C, C), BF16)
    for t in range(3):
        x3[t, X_ZERO] = jnp.zeros((SIDE, C), BF16)
        h3[0, t, H_ZERO] = jnp.zeros((SIDE, C), BF16)
        h3[1, t, H_ZERO] = jnp.zeros((SIDE, C), BF16)
    wown[...] = jnp.zeros(wown.shape, F32)
    wnear[...] = jnp.zeros(wnear.shape, F32)

    def start_of(row, device):
        return jnp.minimum(lax.rem(row - device * SIDE + RIM + 2 * n_total, n_total), 2 * RIM) - RIM

    for c in small_loads:
        c.wait()
    for slot in range(SLOTS):
        own = jnp.where(slot < live_s[0], wts[slot], 0)
        w_send[slot] = own
        wown[slot, 64:128] = own.astype(F32)
    own_starts = [start_of(rows_s[p, 0], me) for p in range(SLOTS)]

    exchanges = []
    for n, (other, at, part) in enumerate(((after, SIDE - 2, RIM), (before, 0, 0))):
        exchanges.append([
            pltpu.make_async_remote_copy(
                src_ref=src, dst_ref=dst, send_sem=send_sem.at[n, m], recv_sem=recv_sem.at[n, m],
                device_id=other, device_id_type=MESH,
            )
            for m, (src, dst) in enumerate((
                (field.at[pl.ds(at, 2)], rim_in.at[n]),
                (w_send.at[:, pl.ds(part, RIM)], w_in.at[n]),
                (rows, rows_in.at[n]),
            ))
        ])

    def send():
        pl.semaphore_wait(barrier, 2)
        for n in range(2):
            for c in exchanges[n]:
                c.start()

    def shift_field(start, count):
        left, _, right = shifts(x3[1, start : start + count].astype(F32))
        x3[0, start : start + count] = left.astype(BF16)
        x3[2, start : start + count] = right.astype(BF16)

    def run_parts(src, first_row, pairs, mirrored):
        return [
            tuple(pair_rows(src[2 - t if mirrored else t, pl.ds(first_row + 2 * p, 2 * pairs)]) for p in range(2))
            for t in range(3)
        ]

    bias_one = b_one[...]
    bias_two = b_two[...]

    def hidden_of(acc):
        h = unpair(acc)
        h = silu(h.reshape(-1, SIDE, C) + bias_one.reshape(1, 1, C))
        return [v.astype(BF16) for v in shifts(h)]

    def first_conv(view, first_row, pairs, mirrored):
        made = hidden_of(pair_dot(run_parts(x3, first_row, pairs, mirrored), wmat, 0))
        for t in range(3):
            h3[view, t, pl.ds(first_row, 2 * pairs)] = made[t]

    def second_conv(view, pair, pairs, mirrored, dst):
        acc = pair_dot(run_parts(h3.at[view], 2 * pair, pairs, mirrored), wmat, 1)
        r = unpair(acc).reshape(2 * pairs, SIDE, C) + bias_two.reshape(1, 1, C)
        dst[pl.ds(2 * pair, 2 * pairs)] = r + x3[1, pl.ds(2 + 2 * pair, 2 * pairs)].astype(F32)

    field_loads[0].wait()
    shift_field(2, 16)
    line_start = lax.rem(me_blk, LINE) == 0
    pl.when(jnp.logical_not(line_start))(send)
    field_loads[1].wait()
    shift_field(18, 16)
    for c in kernel_loads[:2]:
        c.wait()
    first_conv(0, 2, 7, False)
    field_loads[2].wait()
    shift_field(34, 16)
    field_loads[3].wait()
    shift_field(50, 16)
    first_conv(0, 16, 8, False)
    first_conv(0, 32, 8, False)
    first_conv(0, 48, 8, False)
    for c in kernel_loads[2:]:
        c.wait()
    second_conv(0, 1, 8, False, r_main)
    second_conv(0, 9, 8, False, r_main)
    second_conv(0, 17, 8, False, r_main)
    second_conv(0, 25, 6, False, r_main)
    pl.when(jnp.logical_and(line_start, me > 0))(send)

    @pl.when(boundary)
    def _():
        b = jnp.where(me_blk == 0, 0, 15)
        first_conv(1, 2 * (1 + b), 8, True)
        first_conv(1, 2 * (9 + b), 8, True)
        second_conv(1, 1 + b, 8, True, r_turn)
        second_conv(1, 9 + b, 7, True, r_turn)

    def lanes(ref, r):
        return jnp.concatenate([ref(r[0]), ref(r[1])], axis=-1)

    def items_first(items):
        parts = [
            tuple(
                jnp.concatenate([
                    lanes(lambda i: x3[t + m * (2 - 2 * t), i], r[2 * p : 2 * p + 2]) for r, m in items
                ], axis=0)
                for p in range(2)
            )
            for t in range(3)
        ]
        return hidden_of(pair_dot(parts, wmat, 0))

    def items_second(items):
        parts = [
            tuple(
                jnp.concatenate([
                    lanes(lambda i: h3[v, t + m * (2 - 2 * t), i], r[2 * p : 2 * p + 2]) for v, r, m, _ in items
                ], axis=0)
                for p in range(2)
            )
            for t in range(3)
        ]
        r = unpair(pair_dot(parts, wmat, 1)) + bias_two.reshape(1, 1, 1, C)
        return [
            [r[n, q] + x3[1, residual[q]].astype(F32) for q in range(2)]
            for n, (_, _, _, residual) in enumerate(items)
        ]

    own_first, own_second, own_lead, own_weights = [], [], [], []
    for p in range(SLOTS):
        s = own_starts[p]
        e = s + SIDE - 1
        top = s > 0
        own_first.append((
            (jnp.where(top, X_ZERO, e + 1), jnp.where(top, s + 2, e + 2), jnp.where(top, s + 3, X_ZERO), X_ZERO), 0))
        own_second.append((
            0,
            (jnp.where(top, H_ZERO, e - 1), jnp.where(top, H_EDGE + p, e),
             jnp.where(top, s + 2, H_EDGE + p), jnp.where(top, s + 3, H_ZERO)),
            0,
            (jnp.where(top, s + 2, e + 1), jnp.where(top, s + 3, e + 2)),
        ))
        own_lead.append(jnp.where(top, s, e - 1))
        own_weights.append([jnp.where(top, wown[p, 64 + q : 65 + q], wown[p, 126 + q : 127 + q]) for q in range(2)])
    own_first.append(((X_ZERO, 2, 3, X_ZERO), 0))
    own_second.append((0, (H_ZERO, H_EDGE + 3, 2, 3), 0, (2, 3)))
    made = items_first(own_first)
    for t in range(3):
        for n in range(4):
            h3[0, t, H_EDGE + n] = made[t][2 * n]
    own_result = items_second(own_second)
    for n in range(3):
        for q in range(2):
            edge[2 * n + q] = own_result[n][q]
    for q in range(2):
        edge[N_ROWS + q] = own_result[3][q]

    cov[...] = sum(wown[p, pl.ds(64 - own_starts[p], SIDE)] for p in range(SLOTS))
    inner = lax.broadcasted_iota(I32, (SIDE, SIDE), 0)
    within = jnp.logical_and(inner >= 2, inner < SIDE - 2)
    for p in range(SLOTS):
        wown[p, 64:128] = jnp.where(within, wown[p, 64:128], 0.0)
    inside[...] = sum(wown[p, pl.ds(64 - own_starts[p], SIDE)] for p in range(SLOTS))

    def own_at(where, row):
        return sum(
            jnp.where(jnp.logical_and(own_starts[p] == where, p < live_s[0]), wts[p, row : row + 1], 0)
            for p in range(SLOTS)
        ).astype(F32)

    def spread(columns, n):
        return jnp.broadcast_to(columns[:, n : n + 1], (SIDE, C))

    def in_range(row):
        return jnp.logical_and(row >= 0, row < SIDE)

    def coefficients(pairs):
        made = [
            jnp.where(in_range(row), w / cov[pl.ds(jnp.clip(row, 0, SIDE - 1), 1)], 0.0) for w, row in pairs
        ]
        made += [jnp.zeros((1, SIDE), F32)] * (-len(made) % 8)
        return jnp.concatenate(made, axis=0).T

    pl.when(me == 0)(send)

    row_i = lax.broadcasted_iota(I32, (SIDE, SIDE), 0)
    col_i = lax.broadcasted_iota(I32, (SIDE, SIDE), 1)
    indices = [None] * N_ROWS
    writes = []

    def side_of(n):
        flag = (first, last)[n]
        for c in exchanges[n]:
            c.wait_recv()
        turn = jnp.where(flag == 1, SIDE - 1 - col_i, col_i)
        turn = jnp.where(row_i == turn, 1.0, 0.0).astype(BF16)
        rim = jnp.dot(turn, jnp.concatenate([rim_in[n, 0], rim_in[n, 1]], axis=-1), preferred_element_type=F32)
        rim = jnp.stack([rim[:, :C], rim[:, C:]], axis=0)
        for t, v in enumerate(shifts(rim)):
            x3[t, (0, 66)[n] : (2, 68)[n]] = v.astype(BF16)
        starts = [
            start_of(rows_in[n, p, 0], me - 1 if n == 0 else me + 1) + (-SIDE, SIDE)[n] for p in range(SLOTS)
        ]
        pair_first, pair_second = (0, 32)[n], (0, 31)[n]
        items = [
            (tuple(2 * pair_first + j for j in range(4)), 0),
            (tuple(2 * pair_first + j for j in range(4)), flag),
            ((X_ZERO, 1, 2, X_ZERO) if n == 0 else (65, 66, X_ZERO, X_ZERO), 0),
        ]
        static = H_EDGE + 4 + n
        tails = [
            (0, tuple(2 * pair_second + j for j in range(4)), 0, (2 * pair_second + 2, 2 * pair_second + 3)),
            (flag, tuple(2 * pair_second + j for j in range(4)), flag, (2 * pair_second + 2, 2 * pair_second + 3)),
            (0, (H_ZERO, static, 1, 2), 0, (1, 2)) if n == 0 else (0, (63, 64, static, H_ZERO), 0, (65, 66)),
        ]
        for p in range(SLOTS):
            at = H_EDGE + 6 + 3 * n + p
            if n == 0:
                e = jnp.clip(starts[p] + SIDE - 1, 0, RIM - 1)
                items.append(((e + 1, e + 2, X_ZERO, X_ZERO), flag))
                tails.append((flag, (jnp.maximum(e - 1, 0), e, at, H_ZERO), flag, (e + 1, e + 2)))
            else:
                s = jnp.clip(starts[p], RIM, SIDE - 1)
                items.append(((X_ZERO, s + 2, s + 3, X_ZERO), flag))
                tails.append((flag, (H_ZERO, at, s + 2, s + 3), flag, (s + 2, s + 3)))
        made = items_first(items)
        for t in range(3):
            h3[flag, t, 2 * pair_first : 2 * pair_first + 2] = made[t][2:4]
            h3[0, t, 2 * pair_first : 2 * pair_first + 2] = made[t][0:2]
            h3[0, t, static] = made[t][4]
            for p in range(SLOTS):
                h3[flag, t, H_EDGE + 6 + 3 * n + p] = made[t][6 + 2 * p]
        result = items_second(tails)

        w = jnp.dot(
            w_in[n].reshape(SLOTS * RIM, SIDE).astype(F32).astype(BF16), turn, preferred_element_type=F32
        ).reshape(SLOTS, RIM, SIDE)
        inner = lax.broadcasted_iota(I32, w.shape, 1)
        w_inside = jnp.where(inner < RIM - 2, w, 0.0) if n == 0 else jnp.where(inner >= 2, w, 0.0)
        home = (0, 64)[n]
        half = (0, RIM)[n]
        wnear[n, 0, :, home : home + RIM] = w
        wnear[n, 1, :, home : home + RIM] = w_inside
        offsets = [-RIM - starts[p] if n == 0 else 3 * RIM - starts[p] for p in range(SLOTS)]
        cover, near = [
            sum(wnear[n, i, p, pl.ds(offsets[p], RIM)] for p in range(SLOTS)) for i in range(2)
        ]
        cover = cover + cov[half : half + RIM]
        cov[half : half + RIM] = cover
        flag_f = flag.astype(F32)
        plain = (inside[half : half + RIM] + (1.0 - flag_f) * near) / cover
        turned = flag_f * near / cover
        both = jnp.concatenate([plain, turned], axis=0).T

        pairs = []
        for p in range(SLOTS):
            lead = starts[p] + SIDE - 2 if n == 0 else starts[p]
            for q in range(2):
                own_row = RIM - 2 + q if n == 0 else q
                pairs.append((w[p, own_row : own_row + 1], lead + q))
                indices[6 + 6 * n + 2 * p + q] = jnp.clip(lead + q, 0, SIDE - 1)
        if n == 0:
            pairs += [(own_at(-1, 1), 0), (own_at(0, 0), 0), (own_at(0, 1), 1)]
            for p in range(SLOTS):
                for q in range(2):
                    pairs.append((own_weights[p][q], own_lead[p] + q))
                    indices[2 * p + q] = jnp.clip(own_lead[p] + q, 0, SIDE - 1)
        else:
            pairs.append((own_at(1, SIDE - 2), SIDE - 1))
        columns = coefficients(pairs)
        for p in range(SLOTS):
            for q in range(2):
                edge[6 + 6 * n + 2 * p + q] = result[3 + p][q] * spread(columns, 2 * p + q)
        if n == 0:
            for k in range(6):
                edge[k] = edge[k] * spread(columns, 9 + k)
            lane = lax.broadcasted_iota(I32, (8, C), 1)
            packed = jnp.zeros((8, C), I32)
            for k in range(N_ROWS):
                packed = jnp.where(lane == k, indices[k], packed)
            index[...] = packed
            writes.append(pltpu.make_async_copy(edge.at[pl.ds(0, N_ROWS)], edge_out, out_sem.at[0]))
            writes.append(pltpu.make_async_copy(index, index_out, out_sem.at[1]))
            for c in writes[-2:]:
                c.start()
        r_main[2 * pair_second] = result[0][0]
        r_main[2 * pair_second + 1] = result[0][1]
        r_turn[2 * pair_second] = result[1][0]
        r_turn[2 * pair_second + 1] = result[1][1]

        def extra(r):
            if n == 0 and r == 0:
                return result[2][1] * spread(columns, 6) + edge[N_ROWS] * spread(columns, 7)
            if n == 0 and r == 1:
                return edge[N_ROWS + 1] * spread(columns, 8)
            if n == 1 and r == SIDE - 1:
                return result[2][0] * spread(columns, 6)
            return 0.0

        r_extra = {r: extra(r) for r in (0, 1, SIDE - 1) if half <= r < half + RIM}
        for r, v in r_extra.items():
            cov_row = v
            edge[N_ROWS + 2 + (r if r < 2 else 0)] = cov_row

        def fill(turned_too):
            for r in range(half, half + RIM):
                v = r_main[r] * spread(both, r - half)
                if turned_too:
                    v = v + r_turn[r] * spread(both, RIM + r - half)
                if r in r_extra:
                    v = v + edge[N_ROWS + 2 + (r if r < 2 else 0)]
                base[r] = v.astype(BF16)

        pl.when(flag == 0)(functools.partial(fill, False))
        pl.when(flag == 1)(functools.partial(fill, True))
        c = pltpu.make_async_copy(base.at[pl.ds(half, RIM)], base_out.at[pl.ds(half, RIM)], out_sem.at[2 + n])
        c.start()
        writes.append(c)

    side_of(1)
    side_of(0)
    for n in range(2):
        for c in exchanges[n]:
            c.wait_send()
    for c in writes:
        c.wait()


def place(index, base, edge, out, index_s, base_v, edge_v, acc, load_sem, out_sem):
    loads = [
        pltpu.make_async_copy(index, index_s, load_sem.at[0]),
        pltpu.make_async_copy(edge, edge_v, load_sem.at[1]),
        pltpu.make_async_copy(base, base_v, load_sem.at[2]),
    ]
    for c in loads:
        c.start()
    for c in loads:
        c.wait()
    rows = [index_s[0, n] for n in range(N_ROWS)]
    for n in range(N_ROWS):
        acc[rows[n]] = base_v[rows[n]].astype(F32)
    for n in range(N_ROWS):
        acc[rows[n]] += edge_v[n]
    for n in range(N_ROWS):
        base_v[rows[n]] = acc[rows[n]].astype(BF16)
    store = pltpu.make_async_copy(base_v, out, out_sem)
    store.start()
    store.wait()


def shards(field, patch_rows, flips, blend_weights, live, kernel_one, bias_one, kernel_two, bias_two):
    faces, blks = lax.axis_size("face"), lax.axis_size("blk")
    anywhere = pl.BlockSpec(memory_space=pl.ANY)
    vectors = pl.BlockSpec(memory_space=pltpu.VMEM)
    base, edge, index = pl.pallas_call(
        functools.partial(work, faces, blks),
        out_shape=(
            jax.ShapeDtypeStruct((SIDE, SIDE, C), BF16),
            jax.ShapeDtypeStruct((N_ROWS, SIDE, C), F32),
            jax.ShapeDtypeStruct((8, C), I32),
        ),
        in_specs=[anywhere] * 6 + [vectors] * 2,
        out_specs=(anywhere,) * 3,
        scratch_shapes=[
            pltpu.VMEM((3, X_ZERO + 1, SIDE, C), BF16),
            pltpu.VMEM((2, 3, H_EDGE + N_EDGE, SIDE, C), BF16),
            pltpu.VMEM((SIDE, SIDE, C), F32),
            pltpu.VMEM((SIDE, SIDE, C), F32),
            pltpu.VMEM((2, 4, 3, C, 2 * C), BF16),
            pltpu.VMEM((SLOTS, SIDE, SIDE), I32),
            pltpu.VMEM((SLOTS, SIDE, SIDE), I32),
            pltpu.VMEM((2, 2, SIDE, C), BF16),
            pltpu.VMEM((2, SLOTS, RIM, SIDE), I32),
            pltpu.VMEM((2, SLOTS, SIDE), I32),
            pltpu.VMEM((SLOTS, 192, SIDE), F32),
            pltpu.VMEM((2, 2, SLOTS, 96, SIDE), F32),
            pltpu.VMEM((SIDE, SIDE), F32),
            pltpu.VMEM((SIDE, SIDE), F32),
            pltpu.VMEM((SIDE, SIDE, C), BF16),
            pltpu.VMEM((N_ROWS + 4, SIDE, C), F32),
            pltpu.VMEM((8, C), I32),
            pltpu.SMEM((SLOTS, SIDE), I32),
            pltpu.SMEM((1,), I32),
            pltpu.SemaphoreType.DMA((4,)),
            pltpu.SemaphoreType.DMA((7,)),
            pltpu.SemaphoreType.DMA((2, 3)),
            pltpu.SemaphoreType.DMA((2, 3)),
            pltpu.SemaphoreType.DMA((4,)),
        ],
        compiler_params=pltpu.CompilerParams(
            collective_id=0, has_side_effects=True, vmem_limit_bytes=62 * 2**20
        ),
    )(
        field, patch_rows, live, blend_weights, kernel_one, kernel_two,
        bias_one.reshape(1, C), bias_two.reshape(1, C),
    )
    return pl.pallas_call(
        place,
        out_shape=jax.ShapeDtypeStruct((SIDE, SIDE, C), BF16),
        in_specs=[anywhere] * 3,
        out_specs=anywhere,
        scratch_shapes=[
            pltpu.SMEM((8, C), I32),
            pltpu.VMEM((SIDE, SIDE, C), BF16),
            pltpu.VMEM((N_ROWS, SIDE, C), F32),
            pltpu.VMEM((SIDE, SIDE, C), F32),
            pltpu.SemaphoreType.DMA((3,)),
            pltpu.SemaphoreType.DMA,
        ],
        compiler_params=pltpu.CompilerParams(vmem_limit_bytes=62 * 2**20),
    )(index, base, edge)


def solution(mesh):
    split = ("face", "blk")
    placed = (P(split, None, None), P(split, None), P(split, None), P(split, None, None), P(split), P(), P(), P(), P())
    return jax.shard_map(shards, mesh=mesh, in_specs=placed, out_specs=P(split, None, None), check_vma=False)
```

```python
import functools

import jax
import jax.numpy as jnp
from jax import lax
from jax.experimental import pallas as pl
from jax.experimental.pallas import tpu as pltpu
from jax.sharding import PartitionSpec as P

MESH = pl.DeviceIdType.MESH
F32, BF16, I32 = jnp.float32, jnp.bfloat16, jnp.int32
SIDE, C, RIM, SLOTS = 64, 128, 32, 3
X_ZERO = 68
H_ZERO = 66
H_EDGE = 67
N_EDGE = 12
N_ROWS = 18


def shifts(rows):
    column = lax.broadcasted_iota(I32, rows.shape, 1)
    left = jnp.where(column == 0, 0.0, pltpu.roll(rows, 1, 1))
    right = jnp.where(column == SIDE - 1, 0.0, pltpu.roll(rows, SIDE - 1, 1))
    return left, rows, right


def pair_rows(rows):
    n = rows.shape[0] // 2
    rows = rows.reshape(n, 2, SIDE, C)
    return jnp.concatenate([rows[:, 0], rows[:, 1]], axis=-1).reshape(n * SIDE, 2 * C)


def pair_dot(parts, w_ref, conv):
    lhs = jnp.concatenate([parts[t][p] for t in range(3) for p in range(2)], axis=-1)
    rhs = jnp.concatenate(
        [w_ref[conv, 2 * p : 2 * p + 2, t].reshape(2 * C, 2 * C) for t in range(3) for p in range(2)], axis=0
    )
    return jnp.dot(lhs, rhs, preferred_element_type=F32)


def unpair(wide):
    n = wide.shape[0] // SIDE
    return jnp.stack(
        [wide[:, :C].reshape(n, SIDE, C), wide[:, C:].reshape(n, SIDE, C)], axis=1
    )


def silu(z):
    return z * (0.5 + 0.5 * jnp.tanh(0.5 * z))


def work(
    faces, blks,
    field, rows, live, weights, k_one, k_two, b_one, b_two,
    base_out, edge_out, index_out,
    x3, h3, r_all, wmat, wts, w_send, w_in, rim, rim_in, rows_in, wown, cov, base, blend, own_rows, edge, index,
    rows_s, live_s,
    field_sem, load_sem, send_sem, recv_sem, out_sem,
):
    me_face, me_blk = lax.axis_index("face"), lax.axis_index("blk")
    total = faces * blks
    me = me_face * blks + me_blk
    following = lax.rem(me + 1, total)
    preceding = lax.rem(me + total - 1, total)
    after = (following // blks, lax.rem(following, blks))
    before = (preceding // blks, lax.rem(preceding, blks))
    first = jnp.where(me_blk == 0, 1, 0)
    last = jnp.where(me_blk == blks - 1, 1, 0)
    boundary = jnp.logical_or(me_blk == 0, me_blk == blks - 1)
    n_total = total * SIDE

    barrier = pltpu.get_barrier_semaphore()
    for other in (after, before):
        pl.semaphore_signal(barrier, inc=1, device_id=other, device_id_type=MESH)

    small_loads = [
        pltpu.make_async_copy(live, live_s, load_sem.at[5]),
        pltpu.make_async_copy(rows, rows_s, load_sem.at[6]),
        pltpu.make_async_copy(weights, wts, load_sem.at[0]),
        pltpu.make_async_copy(field.at[pl.ds(SIDE - 2, 2)], rim.at[2, pl.ds(0, 2)], load_sem.at[7]),
        pltpu.make_async_copy(field.at[pl.ds(0, 2)], rim.at[2, pl.ds(2, 2)], load_sem.at[8]),
    ]
    field_loads = [
        pltpu.make_async_copy(field.at[pl.ds(16 * n, 16)], x3.at[1, pl.ds(2 + 16 * n, 16)], field_sem.at[n])
        for n in range(4)
    ]
    kernel_loads = [
        pltpu.make_async_copy(
            src, wmat.at[conv, pl.ds(q, 3), :, :, pl.ds(q * C, C)], load_sem.at[1 + 2 * conv + q]
        )
        for conv, src in enumerate((k_one, k_two)) for q in range(2)
    ]
    for c in small_loads + field_loads[:1] + kernel_loads[:2] + field_loads[1:] + kernel_loads[2:]:
        c.start()

    for conv in range(2):
        wmat[conv, 0, :, :, C:] = jnp.zeros((3, C, C), BF16)
        wmat[conv, 3, :, :, :C] = jnp.zeros((3, C, C), BF16)
    for t in range(3):
        x3[t, X_ZERO] = jnp.zeros((SIDE, C), BF16)
        h3[0, t, H_ZERO] = jnp.zeros((SIDE, C), BF16)
        h3[1, t, H_ZERO] = jnp.zeros((SIDE, C), BF16)
    wown[...] = jnp.zeros(wown.shape, F32)

    def start_of(row, device):
        return jnp.minimum(lax.rem(row - device * SIDE + RIM + 2 * n_total, n_total), 2 * RIM) - RIM

    row_i = lax.broadcasted_iota(I32, (SIDE, SIDE), 0)
    col_i = lax.broadcasted_iota(I32, (SIDE, SIDE), 1)

    def prepare(to):
        for slot in range(SLOTS):
            wown[slot, 64:128] = jnp.where(slot < live_s[0], wts[slot], 0).astype(F32)
        for n, flag in enumerate((last, first)):
            turn = jnp.where(flag == 1, SIDE - 1 - col_i, col_i)
            turn = jnp.where(row_i == turn, 1.0, 0.0).astype(BF16)
            pair = jnp.concatenate([rim[2, 2 * n], rim[2, 2 * n + 1]], axis=-1)
            pair = jnp.dot(turn, pair, preferred_element_type=F32).astype(BF16)
            for i in range(2):
                rim[to, 2 * n + i] = pair[:, i * C : i * C + C]
            row = (128, 32)[n]
            line = (126, 64)[n]
            mine = jnp.concatenate(
                [sum(wown[p, pl.ds(row - start_of(rows_s[p, 0], me), RIM)] for p in range(SLOTS))]
                + [wown[p, line : line + 2] for p in range(SLOTS)] + [jnp.zeros((2, SIDE), F32)], axis=0)
            w_send[to, n] = jnp.dot(mine.astype(BF16), turn, preferred_element_type=F32)

    def exchange(n, at):
        return [
            pltpu.make_async_remote_copy(
                src_ref=src, dst_ref=dst, send_sem=send_sem.at[n, m], recv_sem=recv_sem.at[n, m],
                device_id=(after, before)[n], device_id_type=MESH,
            )
            for m, (src, dst) in enumerate((
                (rim.at[at, pl.ds(2 * n, 2)], rim_in.at[n]),
                (w_send.at[at, n], w_in.at[n]),
                (rows, rows_in.at[n]),
            ))
        ]

    exchanges = [exchange(n, 0) for n in range(2)]

    def send(at):
        pl.semaphore_wait(barrier, 2)
        for n in range(2):
            for c in exchange(n, at):
                c.start()

    def shift_field(start, count):
        left, _, right = shifts(x3[1, start : start + count].astype(F32))
        x3[0, start : start + count] = left.astype(BF16)
        x3[2, start : start + count] = right.astype(BF16)

    def stage(body):
        pl.when(me >= 0)(body)

    def run_parts(src, first_row, pairs, mirrored):
        return [
            tuple(pair_rows(src[2 - t if mirrored else t, pl.ds(first_row + 2 * p, 2 * pairs)]) for p in range(2))
            for t in range(3)
        ]

    bias_one = b_one[...]
    bias_two = b_two[...]

    def hidden_of(acc):
        h = unpair(acc)
        h = silu(h.reshape(-1, SIDE, C) + bias_one.reshape(1, 1, C))
        return [v.astype(BF16) for v in shifts(h)]

    def first_conv(view, first_row, pairs, mirrored):
        made = hidden_of(pair_dot(run_parts(x3, first_row, pairs, mirrored), wmat, 0))
        for t in range(3):
            h3[view, t, pl.ds(first_row, 2 * pairs)] = made[t]

    def second_conv(view, pair, pairs, mirrored):
        acc = pair_dot(run_parts(h3.at[view], 2 * pair, pairs, mirrored), wmat, 1)
        r = unpair(acc).reshape(2 * pairs, SIDE, C) + bias_two.reshape(1, 1, C)
        r = r + x3[1, pl.ds(2 + 2 * pair, 2 * pairs)].astype(F32)
        r_all[view, pl.ds(2 * pair, 2 * pairs)] = r
        if view == 0:
            base[pl.ds(2 * pair, 2 * pairs)] = r.astype(BF16)

    @pl.when(me_blk == blks - 1)
    def _():
        for c in small_loads:
            c.wait()
        prepare(0)
        send(0)

    field_loads[0].wait()
    shift_field(2, 16)
    for c in kernel_loads[:2]:
        c.wait()
    first_conv(0, 2, 7, False)

    @pl.when(me_blk < blks - 1)
    def _():
        for c in small_loads:
            c.wait()

    for c in field_loads[1:]:
        c.wait()

    @stage
    def _():
        shift_field(18, 48)
        first_conv(0, 16, 8, False)
        prepare(1)

    pl.when(jnp.logical_and(me_blk > 0, me_blk < blks - 1))(lambda: send(1))

    @stage
    def _():
        first_conv(0, 32, 8, False)
        first_conv(0, 48, 8, False)

    for c in kernel_loads[2:]:
        c.wait()

    @stage
    def _():
        second_conv(0, 1, 8, False)
        second_conv(0, 9, 8, False)
        second_conv(0, 17, 8, False)
        second_conv(0, 25, 6, False)

    writes = []
    for n, flag in enumerate((first, last)):
        bulk = pl.ds((2, RIM)[n], RIM - 2)
        writes.append(pltpu.make_async_copy(base.at[bulk], base_out.at[bulk], out_sem.at[2 + n]))
        pl.when(flag == 0)(writes[n].start)
    pl.when(jnp.logical_and(me_blk == 0, me > 0))(lambda: send(1))

    @pl.when(boundary)
    def _():
        b = jnp.where(me_blk == 0, 0, 15)
        first_conv(1, 2 * (1 + b), 8, True)
        first_conv(1, 2 * (9 + b), 8, True)

    pl.when(me == 0)(lambda: send(1))

    @pl.when(boundary)
    def _():
        b = jnp.where(me_blk == 0, 0, 15)
        second_conv(1, 1 + b, 8, True)
        second_conv(1, 9 + b, 7, True)

    own_starts = [start_of(rows_s[p, 0], me) for p in range(SLOTS)]

    def lanes(ref, r):
        return jnp.concatenate([ref(r[0]), ref(r[1])], axis=-1)

    def items_first(items):
        parts = [
            tuple(
                jnp.concatenate([
                    lanes(lambda i: x3[t + m * (2 - 2 * t), i], r[2 * p : 2 * p + 2]) for r, m in items
                ], axis=0)
                for p in range(2)
            )
            for t in range(3)
        ]
        return hidden_of(pair_dot(parts, wmat, 0))

    def items_second(items):
        parts = [
            tuple(
                jnp.concatenate([
                    lanes(lambda i: h3[v, t + m * (2 - 2 * t), i], r[2 * p : 2 * p + 2]) for v, r, m, _ in items
                ], axis=0)
                for p in range(2)
            )
            for t in range(3)
        ]
        r = unpair(pair_dot(parts, wmat, 1)) + bias_two.reshape(1, 1, 1, C)
        return [
            [r[n, q] + x3[1, residual[q]].astype(F32) for q in range(2)]
            for n, (_, _, _, residual) in enumerate(items)
        ]

    own_first, own_second, own_lead, own_weights = [], [], [], []
    for p in range(SLOTS):
        s = own_starts[p]
        e = s + SIDE - 1
        top = s > 0
        own_first.append((
            (jnp.where(top, X_ZERO, e + 1), jnp.where(top, s + 2, e + 2), jnp.where(top, s + 3, X_ZERO), X_ZERO), 0))
        own_second.append((
            0,
            (jnp.where(top, H_ZERO, e - 1), jnp.where(top, H_EDGE + p, e),
             jnp.where(top, s + 2, H_EDGE + p), jnp.where(top, s + 3, H_ZERO)),
            0,
            (jnp.where(top, s + 2, e + 1), jnp.where(top, s + 3, e + 2)),
        ))
        own_lead.append(jnp.where(top, s, e - 1))
        own_weights.append([jnp.where(top, wown[p, 64 + q : 65 + q], wown[p, 126 + q : 127 + q]) for q in range(2)])
    own_first.append(((X_ZERO, 2, 3, X_ZERO), 0))
    own_second.append((0, (H_ZERO, H_EDGE + 3, 2, 3), 0, (2, 3)))

    @stage
    def _():
        made = items_first(own_first)
        for t in range(3):
            for n in range(4):
                h3[0, t, H_EDGE + n] = made[t][2 * n]

    @stage
    def _():
        own_result = items_second(own_second)
        for n in range(4):
            for q in range(2):
                own_rows[2 * n + q] = own_result[n][q]

    cov[...] = sum(wown[p, pl.ds(64 - own_starts[p], SIDE)] for p in range(SLOTS))

    def own_at(where, row):
        return sum(
            jnp.where(jnp.logical_and(own_starts[p] == where, p < live_s[0]), wts[p, row : row + 1], 0)
            for p in range(SLOTS)
        ).astype(F32)

    def spread(columns, n):
        return jnp.broadcast_to(columns[:, n : n + 1], (SIDE, C))

    def in_range(row):
        return jnp.logical_and(row >= 0, row < SIDE)

    def coefficients(pairs):
        made = [
            jnp.where(in_range(row), w / cov[pl.ds(jnp.clip(row, 0, SIDE - 1), 1)], 0.0) for w, row in pairs
        ]
        made += [jnp.zeros((1, SIDE), F32)] * (-len(made) % 8)
        return jnp.concatenate(made, axis=0).T

    def settle(sides):
        items, tails, starts = [], [], {}
        for n in sides:
            flag = (first, last)[n]
            for c in exchanges[n]:
                c.wait_recv()
            rim_rows = slice((0, 66)[n], (2, 68)[n])
            left, _, right = shifts(rim_in[n].astype(F32))
            x3[1, rim_rows] = rim_in[n]
            x3[0, rim_rows] = left.astype(BF16)
            x3[2, rim_rows] = right.astype(BF16)
            starts[n] = [
                start_of(rows_in[n, p, 0], me - 1 if n == 0 else me + 1) + (-SIDE, SIDE)[n] for p in range(SLOTS)
            ]
            pair_first, pair_second = (0, 32)[n], (0, 31)[n]
            static = H_EDGE + 4 + n
            items += [
                (tuple(2 * pair_first + j for j in range(4)), 0),
                (tuple(2 * pair_first + j for j in range(4)), flag),
                ((X_ZERO, 1, 2, X_ZERO) if n == 0 else (65, 66, X_ZERO, X_ZERO), 0),
            ]
            four = tuple(2 * pair_second + j for j in range(4))
            tails += [
                (0, four, 0, (2 * pair_second + 2, 2 * pair_second + 3)),
                (flag, four, flag, (2 * pair_second + 2, 2 * pair_second + 3)),
                (0, (H_ZERO, static, 1, 2), 0, (1, 2)) if n == 0 else (0, (63, 64, static, H_ZERO), 0, (65, 66)),
            ]
            for p in range(SLOTS):
                at = H_EDGE + 6 + 3 * n + p
                if n == 0:
                    e = jnp.clip(starts[n][p] + SIDE - 1, 0, RIM - 1)
                    items.append(((e + 1, e + 2, X_ZERO, X_ZERO), flag))
                    tails.append((flag, (jnp.maximum(e - 1, 0), e, at, H_ZERO), flag, (e + 1, e + 2)))
                else:
                    s = jnp.clip(starts[n][p], RIM, SIDE - 1)
                    items.append(((X_ZERO, s + 2, s + 3, X_ZERO), flag))
                    tails.append((flag, (H_ZERO, at, s + 2, s + 3), flag, (s + 2, s + 3)))

        @stage
        def _():
            made = items_first(items)
            for k, n in enumerate(sides):
                flag, pair_first = (first, last)[n], (0, 32)[n]
                for t in range(3):
                    m = made[t][12 * k : 12 * k + 12]
                    h3[flag, t, 2 * pair_first : 2 * pair_first + 2] = m[2:4]
                    h3[0, t, 2 * pair_first : 2 * pair_first + 2] = m[0:2]
                    h3[0, t, H_EDGE + 4 + n] = m[4]
                    for p in range(SLOTS):
                        h3[flag, t, H_EDGE + 6 + 3 * n + p] = m[6 + 2 * p]

        @stage
        def _():
            result = items_second(tails)
            for k, n in enumerate(sides):
                finish(n, result[6 * k : 6 * k + 6], starts[n])

        for n in sides:
            bulk = pl.ds((2, RIM)[n], RIM - 2)
            late = pltpu.make_async_copy(blend.at[bulk], base_out.at[bulk], out_sem.at[2 + n])
            pl.when((first, last)[n] == 1)(late.start)

    def finish(n, result, starts):
        flag, half, row = (first, last)[n], (0, RIM)[n], (0, SIDE - 2)[n]
        for view, i in ((flag, 1), (0, 0)):
            for q in range(2):
                r_all[view, row + q] = result[i][q]

        near = w_in[n, 0:RIM]
        cover = cov[half : half + RIM] + near
        cov[half : half + RIM] = cover

        pairs, indices = [], [None] * N_ROWS
        for p in range(SLOTS):
            lead = starts[p] + SIDE - 2 if n == 0 else starts[p]
            for q in range(2):
                k = 2 * p + q
                pairs.append((w_in[n, RIM + k : RIM + k + 1], lead + q))
                indices[6 + 6 * n + k] = jnp.where(in_range(lead + q), lead + q, RIM - 2 + 2 * n + q)
        if n == 0:
            pairs += [(own_at(-1, 1), 0), (own_at(0, 0), 0), (own_at(0, 1), 1)]
            for p in range(SLOTS):
                for q in range(2):
                    pairs.append((own_weights[p][q], own_lead[p] + q))
                    indices[2 * p + q] = own_lead[p] + q
        else:
            pairs.append((own_at(1, SIDE - 2), SIDE - 1))
        columns = coefficients(pairs)
        for k in range(6):
            at = 6 + 6 * n + k
            edge[at] = ((result[3 + k // 2][k % 2] - r_all[flag, indices[at]]) * spread(columns, k)).astype(BF16)
        if n == 0:
            for k in range(6):
                edge[k] = ((own_rows[k] - r_all[0, indices[k]]) * spread(columns, 9 + k)).astype(BF16)
        lane = lax.broadcasted_iota(I32, (8, C), 1)
        packed = index[...] if n == 0 else jnp.zeros((8, C), I32)
        for k in range(N_ROWS):
            if indices[k] is not None:
                packed = jnp.where(lane == k, indices[k], packed)
        index[...] = packed

        share = (near / cover).T
        for r in range(half, half + RIM):
            v = r_all[0, r]
            mixed = v + (r_all[1, r] - v) * spread(share, r - half)
            if row <= r < row + 2:
                base[r] = jnp.where(flag == 1, mixed, v).astype(BF16)
            else:
                blend[r] = mixed.astype(BF16)

        def plus(r, v):
            base[r] = (base[r].astype(F32) + v).astype(BF16)

        if n == 0:
            plus(0, (result[2][1] - result[0][0]) * spread(columns, 6)
                 + (own_rows[6] - result[0][0]) * spread(columns, 7))
            plus(1, (own_rows[7] - result[0][1]) * spread(columns, 8))
        else:
            plus(SIDE - 1, (result[2][0] - result[0][1]) * spread(columns, 6))

    @pl.when(me == 0)
    def _():
        settle((1,))
        settle((0,))

    @pl.when(me > 0)
    def _():
        settle((1, 0))

    tail = [
        pltpu.make_async_copy(edge, edge_out, out_sem.at[0]),
        pltpu.make_async_copy(index, index_out, out_sem.at[1]),
        pltpu.make_async_copy(base.at[pl.ds(0, 2)], base_out.at[pl.ds(0, 2)], out_sem.at[4]),
        pltpu.make_async_copy(base.at[pl.ds(SIDE - 2, 2)], base_out.at[pl.ds(SIDE - 2, 2)], out_sem.at[5]),
    ]
    for c in tail:
        c.start()
    writes += tail
    for n in range(2):
        for c in exchanges[n]:
            c.wait_send()
    for c in writes:
        c.wait()


def place(index, base, edge, out, index_s, base_v, edge_v, load_sem, out_sem):
    loads = [
        pltpu.make_async_copy(index, index_s, load_sem.at[0]),
        pltpu.make_async_copy(edge, edge_v, load_sem.at[1]),
    ] + [
        pltpu.make_async_copy(base.at[pl.ds(16 * n, 16)], base_v.at[pl.ds(16 * n, 16)], load_sem.at[2 + n])
        for n in range(4)
    ]
    for c in loads:
        c.start()
    for c in loads:
        c.wait()
    rows = [index_s[0, n] for n in range(N_ROWS)]
    for n in range(0, N_ROWS, 2):
        v = [(base_v[rows[n + q]].astype(F32) + edge_v[n + q].astype(F32)).astype(BF16) for q in range(2)]
        for q in range(2):
            base_v[rows[n + q]] = v[q]
    stores = [
        pltpu.make_async_copy(base_v.at[pl.ds(16 * n, 16)], out.at[pl.ds(16 * n, 16)], out_sem.at[n]) for n in range(4)
    ]
    for c in stores:
        c.start()
    for c in stores:
        c.wait()


def shards(field, patch_rows, flips, blend_weights, live, kernel_one, bias_one, kernel_two, bias_two):
    faces, blks = lax.axis_size("face"), lax.axis_size("blk")
    anywhere = pl.BlockSpec(memory_space=pl.ANY)
    vectors = pl.BlockSpec(memory_space=pltpu.VMEM)
    far = pl.BlockSpec(memory_space=pltpu.HBM)
    base, edge, index = pl.pallas_call(
        functools.partial(work, faces, blks),
        out_shape=(
            jax.ShapeDtypeStruct((SIDE, SIDE, C), BF16),
            jax.ShapeDtypeStruct((N_ROWS, SIDE, C), BF16),
            jax.ShapeDtypeStruct((8, C), I32),
        ),
        in_specs=[anywhere, anywhere, far, anywhere, anywhere, anywhere, vectors, vectors],
        out_specs=(anywhere,) * 3,
        scratch_shapes=[
            pltpu.VMEM((3, X_ZERO + 1, SIDE, C), BF16),
            pltpu.VMEM((2, 3, H_EDGE + N_EDGE, SIDE, C), BF16),
            pltpu.VMEM((2, SIDE, SIDE, C), F32),
            pltpu.VMEM((2, 4, 3, C, 2 * C), BF16),
            pltpu.VMEM((SLOTS, SIDE, SIDE), I32),
            pltpu.VMEM((2, 2, 40, SIDE), F32),
            pltpu.VMEM((2, 40, SIDE), F32),
            pltpu.VMEM((3, 4, SIDE, C), BF16),
            pltpu.VMEM((2, 2, SIDE, C), BF16),
            pltpu.VMEM((2, SLOTS, SIDE), I32),
            pltpu.VMEM((SLOTS, 192, SIDE), F32),
            pltpu.VMEM((SIDE, SIDE), F32),
            pltpu.VMEM((SIDE, SIDE, C), BF16),
            pltpu.VMEM((SIDE, SIDE, C), BF16),
            pltpu.VMEM((8, SIDE, C), F32),
            pltpu.VMEM((N_ROWS, SIDE, C), BF16),
            pltpu.VMEM((8, C), I32),
            pltpu.SMEM((SLOTS, SIDE), I32),
            pltpu.SMEM((1,), I32),
            pltpu.SemaphoreType.DMA((4,)),
            pltpu.SemaphoreType.DMA((9,)),
            pltpu.SemaphoreType.DMA((2, 3)),
            pltpu.SemaphoreType.DMA((2, 3)),
            pltpu.SemaphoreType.DMA((6,)),
        ],
        compiler_params=pltpu.CompilerParams(
            collective_id=0, has_side_effects=True, vmem_limit_bytes=62 * 2**20
        ),
    )(
        field, patch_rows, live, blend_weights, kernel_one, kernel_two,
        bias_one.reshape(1, C), bias_two.reshape(1, C),
    )
    return pl.pallas_call(
        place,
        out_shape=jax.ShapeDtypeStruct((SIDE, SIDE, C), BF16),
        in_specs=[anywhere] * 3,
        out_specs=anywhere,
        scratch_shapes=[
            pltpu.SMEM((8, C), I32),
            pltpu.VMEM((SIDE, SIDE, C), BF16),
            pltpu.VMEM((N_ROWS, SIDE, C), BF16),
            pltpu.SemaphoreType.DMA((6,)),
            pltpu.SemaphoreType.DMA((4,)),
        ],
        compiler_params=pltpu.CompilerParams(vmem_limit_bytes=62 * 2**20),
    )(index, base, edge)


def solution(mesh):
    split = ("face", "blk")
    placed = (P(split, None, None), P(split, None), P(split, None), P(split, None, None), P(split), P(), P(), P(), P())
    return jax.shard_map(shards, mesh=mesh, in_specs=placed, out_specs=P(split, None, None), check_vma=False)
```

```python
import functools

import jax
import jax.numpy as jnp
from jax import lax
from jax.experimental import pallas as pl
from jax.experimental.pallas import tpu as pltpu
from jax.sharding import PartitionSpec as P

MESH = pl.DeviceIdType.MESH
F32, BF16, I32 = jnp.float32, jnp.bfloat16, jnp.int32
SIDE, C, RIM, SLOTS = 64, 128, 32, 3
X_ZERO = 68
H_ZERO = 66
H_EDGE = 67
N_EDGE = 12
N_ROWS = 18


def shifts(rows):
    column = lax.broadcasted_iota(I32, rows.shape, 1)
    left = jnp.where(column == 0, 0.0, pltpu.roll(rows, 1, 1))
    right = jnp.where(column == SIDE - 1, 0.0, pltpu.roll(rows, SIDE - 1, 1))
    return left, rows, right


def pair_rows(rows):
    n = rows.shape[0] // 2
    rows = rows.reshape(n, 2, SIDE, C)
    return jnp.concatenate([rows[:, 0], rows[:, 1]], axis=-1).reshape(n * SIDE, 2 * C)


def pair_dot(parts, w_ref, conv):
    lhs = jnp.concatenate([parts[t][p] for t in range(3) for p in range(2)], axis=-1)
    rhs = jnp.concatenate(
        [w_ref[conv, 2 * p : 2 * p + 2, t].reshape(2 * C, 2 * C) for t in range(3) for p in range(2)], axis=0
    )
    return jnp.dot(lhs, rhs, preferred_element_type=F32)


def unpair(wide):
    n = wide.shape[0] // SIDE
    return jnp.stack(
        [wide[:, :C].reshape(n, SIDE, C), wide[:, C:].reshape(n, SIDE, C)], axis=1
    )


def silu(z):
    return z * (0.5 + 0.5 * jnp.tanh(0.5 * z))


def work(
    faces, blks,
    field, rows, live, weights, k_one, k_two, b_one, b_two,
    base_out, edge_out, index_out,
    x3, h3, r_all, wmat, wts, w_send, w_in, rim, rim_in, rows_in, wown, cov, base, blend, own_rows, edge, index,
    bias, rows_s, live_s,
    field_sem, load_sem, send_sem, recv_sem, out_sem,
):
    me_face, me_blk = lax.axis_index("face"), lax.axis_index("blk")
    total = faces * blks
    me = me_face * blks + me_blk
    following = lax.rem(me + 1, total)
    preceding = lax.rem(me + total - 1, total)
    after = (following // blks, lax.rem(following, blks))
    before = (preceding // blks, lax.rem(preceding, blks))
    first = jnp.where(me_blk == 0, 1, 0)
    last = jnp.where(me_blk == blks - 1, 1, 0)
    boundary = jnp.logical_or(me_blk == 0, me_blk == blks - 1)
    n_total = total * SIDE

    barrier = pltpu.get_barrier_semaphore()
    for other in (after, before):
        pl.semaphore_signal(barrier, inc=1, device_id=other, device_id_type=MESH)

    small_loads = [
        pltpu.make_async_copy(live, live_s, load_sem.at[5]),
        pltpu.make_async_copy(rows, rows_s, load_sem.at[6]),
        pltpu.make_async_copy(weights, wts, load_sem.at[0]),
        pltpu.make_async_copy(field.at[pl.ds(SIDE - 2, 2)], rim.at[2, pl.ds(0, 2)], load_sem.at[7]),
        pltpu.make_async_copy(field.at[pl.ds(0, 2)], rim.at[2, pl.ds(2, 2)], load_sem.at[8]),
    ]
    field_loads = [
        pltpu.make_async_copy(field.at[pl.ds(16 * n, 16)], x3.at[1, pl.ds(2 + 16 * n, 16)], field_sem.at[n])
        for n in range(4)
    ]
    kernel_loads = [
        pltpu.make_async_copy(
            src, wmat.at[conv, pl.ds(q, 3), :, :, pl.ds(q * C, C)], load_sem.at[1 + 2 * conv + q]
        )
        for conv, src in enumerate((k_one, k_two)) for q in range(2)
    ]
    bias_loads = [
        pltpu.make_async_copy(src, bias.at[conv], load_sem.at[9 + conv]) for conv, src in enumerate((b_one, b_two))
    ]
    early = field_loads[:1] + kernel_loads[:2] + bias_loads[:1]

    def start(copies):
        for c in copies:
            c.start()

    pl.when(me_blk == blks - 1)(lambda: start(small_loads + early))
    pl.when(me_blk < blks - 1)(lambda: start(early + small_loads))
    start(field_loads[1:] + kernel_loads[2:] + bias_loads[1:])

    for conv in range(2):
        wmat[conv, 0, :, :, C:] = jnp.zeros((3, C, C), BF16)
        wmat[conv, 3, :, :, :C] = jnp.zeros((3, C, C), BF16)
    for t in range(3):
        x3[t, X_ZERO] = jnp.zeros((SIDE, C), BF16)
        h3[0, t, H_ZERO] = jnp.zeros((SIDE, C), BF16)
        h3[1, t, H_ZERO] = jnp.zeros((SIDE, C), BF16)
    wown[...] = jnp.zeros(wown.shape, F32)

    def start_of(row, device):
        return jnp.minimum(lax.rem(row - device * SIDE + RIM + 2 * n_total, n_total), 2 * RIM) - RIM

    row_i = lax.broadcasted_iota(I32, (SIDE, SIDE), 0)
    col_i = lax.broadcasted_iota(I32, (SIDE, SIDE), 1)

    def prepare(to):
        for slot in range(SLOTS):
            wown[slot, 64:128] = jnp.where(slot < live_s[0], wts[slot], 0).astype(F32)
        for n, flag in enumerate((last, first)):
            turn = jnp.where(flag == 1, SIDE - 1 - col_i, col_i)
            turn = jnp.where(row_i == turn, 1.0, 0.0).astype(BF16)
            pair = jnp.concatenate([rim[2, 2 * n], rim[2, 2 * n + 1]], axis=-1)
            pair = jnp.dot(turn, pair, preferred_element_type=F32).astype(BF16)
            for i in range(2):
                rim[to, 2 * n + i] = pair[:, i * C : i * C + C]
            row = (128, 32)[n]
            line = (126, 64)[n]
            mine = jnp.concatenate(
                [sum(wown[p, pl.ds(row - start_of(rows_s[p, 0], me), RIM)] for p in range(SLOTS))]
                + [wown[p, line : line + 2] for p in range(SLOTS)] + [jnp.zeros((2, SIDE), F32)], axis=0)
            w_send[to, n] = jnp.dot(mine.astype(BF16), turn, preferred_element_type=F32)

    def exchange(n, at):
        return [
            pltpu.make_async_remote_copy(
                src_ref=src, dst_ref=dst, send_sem=send_sem.at[n, m], recv_sem=recv_sem.at[n, m],
                device_id=(after, before)[n], device_id_type=MESH,
            )
            for m, (src, dst) in enumerate((
                (rim.at[at, pl.ds(2 * n, 2)], rim_in.at[n]),
                (w_send.at[at, n], w_in.at[n]),
                (rows, rows_in.at[n]),
            ))
        ]

    exchanges = [exchange(n, 0) for n in range(2)]

    def send(at):
        pl.semaphore_wait(barrier, 2)
        for n in range(2):
            for c in exchange(n, at):
                c.start()

    def shift_field(start, count):
        left, _, right = shifts(x3[1, start : start + count].astype(F32))
        x3[0, start : start + count] = left.astype(BF16)
        x3[2, start : start + count] = right.astype(BF16)

    def stage(body):
        pl.when(me >= 0)(body)

    def run_parts(src, first_row, pairs, mirrored):
        return [
            tuple(pair_rows(src[2 - t if mirrored else t, pl.ds(first_row + 2 * p, 2 * pairs)]) for p in range(2))
            for t in range(3)
        ]


    def hidden_of(acc):
        h = unpair(acc)
        h = silu(h.reshape(-1, SIDE, C) + bias[0].reshape(1, 1, C))
        return [v.astype(BF16) for v in shifts(h)]

    def first_conv(view, first_row, pairs, mirrored):
        made = hidden_of(pair_dot(run_parts(x3, first_row, pairs, mirrored), wmat, 0))
        for t in range(3):
            h3[view, t, pl.ds(first_row, 2 * pairs)] = made[t]

    def second_conv(view, pair, pairs, mirrored):
        acc = pair_dot(run_parts(h3.at[view], 2 * pair, pairs, mirrored), wmat, 1)
        r = unpair(acc).reshape(2 * pairs, SIDE, C) + bias[1].reshape(1, 1, C)
        r = r + x3[1, pl.ds(2 + 2 * pair, 2 * pairs)].astype(F32)
        r_all[view, pl.ds(2 * pair, 2 * pairs)] = r
        if view == 0:
            base[pl.ds(2 * pair, 2 * pairs)] = r.astype(BF16)

    @pl.when(me_blk == blks - 1)
    def _():
        for c in small_loads:
            c.wait()
        prepare(0)
        send(0)

    field_loads[0].wait()
    shift_field(2, 16)
    for c in kernel_loads[:2] + bias_loads[:1]:
        c.wait()
    first_conv(0, 2, 7, False)

    @pl.when(me_blk < blks - 1)
    def _():
        for c in small_loads:
            c.wait()

    for c in field_loads[1:]:
        c.wait()

    @stage
    def _():
        shift_field(18, 48)
        first_conv(0, 16, 8, False)
        prepare(1)

    pl.when(jnp.logical_and(me_blk > 0, me_blk < blks - 1))(lambda: send(1))

    @stage
    def _():
        first_conv(0, 32, 8, False)
        first_conv(0, 48, 8, False)

    for c in kernel_loads[2:] + bias_loads[1:]:
        c.wait()

    @stage
    def _():
        second_conv(0, 1, 8, False)
        second_conv(0, 9, 8, False)
        second_conv(0, 17, 8, False)
        second_conv(0, 25, 6, False)

    writes = []
    for n, flag in enumerate((first, last)):
        bulk = pl.ds((2, RIM)[n], RIM - 2)
        writes.append(pltpu.make_async_copy(base.at[bulk], base_out.at[bulk], out_sem.at[2 + n]))
        pl.when(flag == 0)(writes[n].start)
    pl.when(jnp.logical_and(me_blk == 0, me > 0))(lambda: send(1))

    @pl.when(boundary)
    def _():
        b = jnp.where(me_blk == 0, 0, 15)
        first_conv(1, 2 * (1 + b), 8, True)
        first_conv(1, 2 * (9 + b), 8, True)

    pl.when(me == 0)(lambda: send(1))

    @pl.when(boundary)
    def _():
        b = jnp.where(me_blk == 0, 0, 15)
        second_conv(1, 1 + b, 8, True)
        second_conv(1, 9 + b, 7, True)

    own_starts = [start_of(rows_s[p, 0], me) for p in range(SLOTS)]

    def lanes(ref, r):
        return jnp.concatenate([ref(r[0]), ref(r[1])], axis=-1)

    def items_first(items):
        parts = [
            tuple(
                jnp.concatenate([
                    lanes(lambda i: x3[t + m * (2 - 2 * t), i], r[2 * p : 2 * p + 2]) for r, m in items
                ], axis=0)
                for p in range(2)
            )
            for t in range(3)
        ]
        return hidden_of(pair_dot(parts, wmat, 0))

    def items_second(items):
        parts = [
            tuple(
                jnp.concatenate([
                    lanes(lambda i: h3[v, t + m * (2 - 2 * t), i], r[2 * p : 2 * p + 2]) for v, r, m, _ in items
                ], axis=0)
                for p in range(2)
            )
            for t in range(3)
        ]
        r = unpair(pair_dot(parts, wmat, 1)) + bias[1].reshape(1, 1, 1, C)
        return [
            [r[n, q] + x3[1, residual[q]].astype(F32) for q in range(2)]
            for n, (_, _, _, residual) in enumerate(items)
        ]

    own_first, own_second, own_lead, own_weights = [], [], [], []
    for p in range(SLOTS):
        s = own_starts[p]
        e = s + SIDE - 1
        top = s > 0
        own_first.append((
            (jnp.where(top, X_ZERO, e + 1), jnp.where(top, s + 2, e + 2), jnp.where(top, s + 3, X_ZERO), X_ZERO), 0))
        own_second.append((
            0,
            (jnp.where(top, H_ZERO, e - 1), jnp.where(top, H_EDGE + p, e),
             jnp.where(top, s + 2, H_EDGE + p), jnp.where(top, s + 3, H_ZERO)),
            0,
            (jnp.where(top, s + 2, e + 1), jnp.where(top, s + 3, e + 2)),
        ))
        own_lead.append(jnp.where(top, s, e - 1))
        own_weights.append([jnp.where(top, wown[p, 64 + q : 65 + q], wown[p, 126 + q : 127 + q]) for q in range(2)])
    own_first.append(((X_ZERO, 2, 3, X_ZERO), 0))
    own_second.append((0, (H_ZERO, H_EDGE + 3, 2, 3), 0, (2, 3)))

    @stage
    def _():
        made = items_first(own_first)
        for t in range(3):
            for n in range(4):
                h3[0, t, H_EDGE + n] = made[t][2 * n]

    @stage
    def _():
        own_result = items_second(own_second)
        for n in range(4):
            for q in range(2):
                own_rows[2 * n + q] = own_result[n][q]

    cov[...] = sum(wown[p, pl.ds(64 - own_starts[p], SIDE)] for p in range(SLOTS))

    def own_at(where, row):
        return sum(
            jnp.where(jnp.logical_and(own_starts[p] == where, p < live_s[0]), wts[p, row : row + 1], 0)
            for p in range(SLOTS)
        ).astype(F32)

    def spread(columns, n):
        return jnp.broadcast_to(columns[:, n : n + 1], (SIDE, C))

    def in_range(row):
        return jnp.logical_and(row >= 0, row < SIDE)

    def coefficients(pairs):
        made = [
            jnp.where(in_range(row), w / cov[pl.ds(jnp.clip(row, 0, SIDE - 1), 1)], 0.0) for w, row in pairs
        ]
        made += [jnp.zeros((1, SIDE), F32)] * (-len(made) % 8)
        return jnp.concatenate(made, axis=0).T

    def settle(sides):
        items, tails, starts = [], [], {}
        for n in sides:
            flag = (first, last)[n]
            for c in exchanges[n]:
                c.wait_recv()
            rim_rows = slice((0, 66)[n], (2, 68)[n])
            left, _, right = shifts(rim_in[n].astype(F32))
            x3[1, rim_rows] = rim_in[n]
            x3[0, rim_rows] = left.astype(BF16)
            x3[2, rim_rows] = right.astype(BF16)
            starts[n] = [
                start_of(rows_in[n, p, 0], me - 1 if n == 0 else me + 1) + (-SIDE, SIDE)[n] for p in range(SLOTS)
            ]
            pair_first, pair_second = (0, 32)[n], (0, 31)[n]
            static = H_EDGE + 4 + n
            items += [
                (tuple(2 * pair_first + j for j in range(4)), 0),
                (tuple(2 * pair_first + j for j in range(4)), flag),
                ((X_ZERO, 1, 2, X_ZERO) if n == 0 else (65, 66, X_ZERO, X_ZERO), 0),
            ]
            four = tuple(2 * pair_second + j for j in range(4))
            tails += [
                (0, four, 0, (2 * pair_second + 2, 2 * pair_second + 3)),
                (flag, four, flag, (2 * pair_second + 2, 2 * pair_second + 3)),
                (0, (H_ZERO, static, 1, 2), 0, (1, 2)) if n == 0 else (0, (63, 64, static, H_ZERO), 0, (65, 66)),
            ]
            for p in range(SLOTS):
                at = H_EDGE + 6 + 3 * n + p
                if n == 0:
                    e = jnp.clip(starts[n][p] + SIDE - 1, 0, RIM - 1)
                    items.append(((e + 1, e + 2, X_ZERO, X_ZERO), flag))
                    tails.append((flag, (jnp.maximum(e - 1, 0), e, at, H_ZERO), flag, (e + 1, e + 2)))
                else:
                    s = jnp.clip(starts[n][p], RIM, SIDE - 1)
                    items.append(((X_ZERO, s + 2, s + 3, X_ZERO), flag))
                    tails.append((flag, (H_ZERO, at, s + 2, s + 3), flag, (s + 2, s + 3)))

        @stage
        def _():
            made = items_first(items)
            for k, n in enumerate(sides):
                flag, pair_first = (first, last)[n], (0, 32)[n]
                for t in range(3):
                    m = made[t][12 * k : 12 * k + 12]
                    h3[flag, t, 2 * pair_first : 2 * pair_first + 2] = m[2:4]
                    h3[0, t, 2 * pair_first : 2 * pair_first + 2] = m[0:2]
                    h3[0, t, H_EDGE + 4 + n] = m[4]
                    for p in range(SLOTS):
                        h3[flag, t, H_EDGE + 6 + 3 * n + p] = m[6 + 2 * p]

        @stage
        def _():
            result = items_second(tails)
            for k, n in enumerate(sides):
                finish(n, result[6 * k : 6 * k + 6], starts[n])

        for n in sides:
            bulk = pl.ds((2, RIM)[n], RIM - 2)
            late = pltpu.make_async_copy(blend.at[bulk], base_out.at[bulk], out_sem.at[2 + n])
            pl.when((first, last)[n] == 1)(late.start)

    def finish(n, result, starts):
        flag, half, row = (first, last)[n], (0, RIM)[n], (0, SIDE - 2)[n]
        for view, i in ((flag, 1), (0, 0)):
            for q in range(2):
                r_all[view, row + q] = result[i][q]

        near = w_in[n, 0:RIM]
        cover = cov[half : half + RIM] + near
        cov[half : half + RIM] = cover

        pairs, indices = [], [None] * N_ROWS
        for p in range(SLOTS):
            lead = starts[p] + SIDE - 2 if n == 0 else starts[p]
            for q in range(2):
                k = 2 * p + q
                pairs.append((w_in[n, RIM + k : RIM + k + 1], lead + q))
                indices[6 + 6 * n + k] = jnp.where(in_range(lead + q), lead + q, RIM - 2 + 2 * n + q)
        if n == 0:
            pairs += [(own_at(-1, 1), 0), (own_at(0, 0), 0), (own_at(0, 1), 1)]
            for p in range(SLOTS):
                for q in range(2):
                    pairs.append((own_weights[p][q], own_lead[p] + q))
                    indices[2 * p + q] = own_lead[p] + q
        else:
            pairs.append((own_at(1, SIDE - 2), SIDE - 1))
        columns = coefficients(pairs)
        for k in range(6):
            at = 6 + 6 * n + k
            edge[at] = ((result[3 + k // 2][k % 2] - r_all[flag, indices[at]]) * spread(columns, k)).astype(BF16)
        if n == 0:
            for k in range(6):
                edge[k] = ((own_rows[k] - r_all[0, indices[k]]) * spread(columns, 9 + k)).astype(BF16)
        lane = lax.broadcasted_iota(I32, (8, C), 1)
        packed = index[...] if n == 0 else jnp.zeros((8, C), I32)
        for k in range(N_ROWS):
            if indices[k] is not None:
                packed = jnp.where(lane == k, indices[k], packed)
        index[...] = packed

        share = (near / cover).T
        for r in range(half, half + RIM):
            v = r_all[0, r]
            mixed = v + (r_all[1, r] - v) * spread(share, r - half)
            if row <= r < row + 2:
                base[r] = jnp.where(flag == 1, mixed, v).astype(BF16)
            else:
                blend[r] = mixed.astype(BF16)

        def plus(r, v):
            base[r] = (base[r].astype(F32) + v).astype(BF16)

        if n == 0:
            plus(0, (result[2][1] - result[0][0]) * spread(columns, 6)
                 + (own_rows[6] - result[0][0]) * spread(columns, 7))
            plus(1, (own_rows[7] - result[0][1]) * spread(columns, 8))
        else:
            plus(SIDE - 1, (result[2][0] - result[0][1]) * spread(columns, 6))

    @pl.when(me == 0)
    def _():
        settle((1,))
        settle((0,))

    @pl.when(me > 0)
    def _():
        settle((1, 0))

    tail = [
        pltpu.make_async_copy(edge, edge_out, out_sem.at[0]),
        pltpu.make_async_copy(index, index_out, out_sem.at[1]),
        pltpu.make_async_copy(base.at[pl.ds(0, 2)], base_out.at[pl.ds(0, 2)], out_sem.at[4]),
        pltpu.make_async_copy(base.at[pl.ds(SIDE - 2, 2)], base_out.at[pl.ds(SIDE - 2, 2)], out_sem.at[5]),
    ]
    for c in tail:
        c.start()
    writes += tail
    for n in range(2):
        for c in exchanges[n]:
            c.wait_send()
    for c in writes:
        c.wait()


def place(index, base, edge, out, index_s, base_v, edge_v, load_sem, out_sem):
    loads = [
        pltpu.make_async_copy(index, index_s, load_sem.at[0]),
        pltpu.make_async_copy(edge, edge_v, load_sem.at[1]),
    ] + [
        pltpu.make_async_copy(base.at[pl.ds(16 * n, 16)], base_v.at[pl.ds(16 * n, 16)], load_sem.at[2 + n])
        for n in range(4)
    ]
    for c in loads:
        c.start()
    for c in loads:
        c.wait()
    rows = [index_s[0, n] for n in range(N_ROWS)]
    for n in range(0, N_ROWS, 2):
        v = [(base_v[rows[n + q]].astype(F32) + edge_v[n + q].astype(F32)).astype(BF16) for q in range(2)]
        for q in range(2):
            base_v[rows[n + q]] = v[q]
    stores = [
        pltpu.make_async_copy(base_v.at[pl.ds(16 * n, 16)], out.at[pl.ds(16 * n, 16)], out_sem.at[n]) for n in range(4)
    ]
    for c in stores:
        c.start()
    for c in stores:
        c.wait()


def shards(field, patch_rows, flips, blend_weights, live, kernel_one, bias_one, kernel_two, bias_two):
    faces, blks = lax.axis_size("face"), lax.axis_size("blk")
    anywhere = pl.BlockSpec(memory_space=pl.ANY)
    base, edge, index = pl.pallas_call(
        functools.partial(work, faces, blks),
        out_shape=(
            jax.ShapeDtypeStruct((SIDE, SIDE, C), BF16),
            jax.ShapeDtypeStruct((N_ROWS, SIDE, C), BF16),
            jax.ShapeDtypeStruct((8, C), I32),
        ),
        in_specs=[anywhere] * 8,
        out_specs=(anywhere,) * 3,
        scratch_shapes=[
            pltpu.VMEM((3, X_ZERO + 1, SIDE, C), BF16),
            pltpu.VMEM((2, 3, H_EDGE + N_EDGE, SIDE, C), BF16),
            pltpu.VMEM((2, SIDE, SIDE, C), F32),
            pltpu.VMEM((2, 4, 3, C, 2 * C), BF16),
            pltpu.VMEM((SLOTS, SIDE, SIDE), I32),
            pltpu.VMEM((2, 2, 40, SIDE), F32),
            pltpu.VMEM((2, 40, SIDE), F32),
            pltpu.VMEM((3, 4, SIDE, C), BF16),
            pltpu.VMEM((2, 2, SIDE, C), BF16),
            pltpu.VMEM((2, SLOTS, SIDE), I32),
            pltpu.VMEM((SLOTS, 192, SIDE), F32),
            pltpu.VMEM((SIDE, SIDE), F32),
            pltpu.VMEM((SIDE, SIDE, C), BF16),
            pltpu.VMEM((SIDE, SIDE, C), BF16),
            pltpu.VMEM((8, SIDE, C), F32),
            pltpu.VMEM((N_ROWS, SIDE, C), BF16),
            pltpu.VMEM((8, C), I32),
            pltpu.VMEM((2, 1, C), F32),
            pltpu.SMEM((SLOTS, SIDE), I32),
            pltpu.SMEM((1,), I32),
            pltpu.SemaphoreType.DMA((4,)),
            pltpu.SemaphoreType.DMA((11,)),
            pltpu.SemaphoreType.DMA((2, 3)),
            pltpu.SemaphoreType.DMA((2, 3)),
            pltpu.SemaphoreType.DMA((6,)),
        ],
        compiler_params=pltpu.CompilerParams(
            collective_id=0, has_side_effects=True, vmem_limit_bytes=62 * 2**20
        ),
    )(
        field, patch_rows, live, blend_weights, kernel_one, kernel_two,
        bias_one.reshape(1, C), bias_two.reshape(1, C),
    )
    return pl.pallas_call(
        place,
        out_shape=jax.ShapeDtypeStruct((SIDE, SIDE, C), BF16),
        in_specs=[anywhere] * 3,
        out_specs=anywhere,
        scratch_shapes=[
            pltpu.SMEM((8, C), I32),
            pltpu.VMEM((SIDE, SIDE, C), BF16),
            pltpu.VMEM((N_ROWS, SIDE, C), BF16),
            pltpu.SemaphoreType.DMA((6,)),
            pltpu.SemaphoreType.DMA((4,)),
        ],
        compiler_params=pltpu.CompilerParams(vmem_limit_bytes=62 * 2**20),
    )(index, base, edge)


def solution(mesh):
    split = ("face", "blk")
    placed = (P(split, None, None), P(split, None), P(split, None), P(split, None, None), P(split), P(), P(), P(), P())
    return jax.shard_map(shards, mesh=mesh, in_specs=placed, out_specs=P(split, None, None), check_vma=False)
```

```python
import functools

import jax
import jax.numpy as jnp
from jax import lax
from jax.experimental import pallas as pl
from jax.experimental.pallas import tpu as pltpu
from jax.sharding import PartitionSpec as P

MESH = pl.DeviceIdType.MESH
F32, BF16, I32 = jnp.float32, jnp.bfloat16, jnp.int32
SIDE, C, RIM, SLOTS = 64, 128, 32, 3
X_ZERO = 68
H_ZERO = 66
H_EDGE = 67
N_EDGE = 12
N_ROWS = 18


def shifts(rows):
    column = lax.broadcasted_iota(I32, rows.shape, 1)
    left = jnp.where(column == 0, 0.0, pltpu.roll(rows, 1, 1))
    right = jnp.where(column == SIDE - 1, 0.0, pltpu.roll(rows, SIDE - 1, 1))
    return left, rows, right


def pair_rows(rows):
    n = rows.shape[0] // 2
    rows = rows.reshape(n, 2, SIDE, C)
    return jnp.concatenate([rows[:, 0], rows[:, 1]], axis=-1).reshape(n * SIDE, 2 * C)


def pair_dot(parts, w_ref, conv):
    lhs = jnp.concatenate([parts[t][p] for t in range(3) for p in range(2)], axis=-1)
    rhs = jnp.concatenate(
        [w_ref[conv, 2 * p : 2 * p + 2, t].reshape(2 * C, 2 * C) for t in range(3) for p in range(2)], axis=0
    )
    return jnp.dot(lhs, rhs, preferred_element_type=F32)


def unpair(wide):
    n = wide.shape[0] // SIDE
    return jnp.stack(
        [wide[:, :C].reshape(n, SIDE, C), wide[:, C:].reshape(n, SIDE, C)], axis=1
    )


def silu(z):
    return z * (0.5 + 0.5 * jnp.tanh(0.5 * z))


def work(
    faces, blks,
    field, rows, live, weights, k_one, k_two, b_one, b_two,
    base_out, edge_out, index_out,
    x3, h3, r_all, wmat, wts, w_send, w_in, rim, rim_in, rows_in, wown, cov, base, blend, own_rows, edge, index,
    bias, rows_s, live_s,
    field_sem, load_sem, send_sem, recv_sem, out_sem,
):
    me_face, me_blk = lax.axis_index("face"), lax.axis_index("blk")
    total = faces * blks
    me = me_face * blks + me_blk
    following = lax.rem(me + 1, total)
    preceding = lax.rem(me + total - 1, total)
    after = (following // blks, lax.rem(following, blks))
    before = (preceding // blks, lax.rem(preceding, blks))
    first = jnp.where(me_blk == 0, 1, 0)
    last = jnp.where(me_blk == blks - 1, 1, 0)
    boundary = jnp.logical_or(me_blk == 0, me_blk == blks - 1)
    n_total = total * SIDE

    barrier = pltpu.get_barrier_semaphore()
    for other in (after, before):
        pl.semaphore_signal(barrier, inc=1, device_id=other, device_id_type=MESH)

    small_loads = [
        pltpu.make_async_copy(live, live_s, load_sem.at[5]),
        pltpu.make_async_copy(rows, rows_s, load_sem.at[6]),
        pltpu.make_async_copy(weights, wts, load_sem.at[0]),
        pltpu.make_async_copy(field.at[pl.ds(SIDE - 2, 2)], rim.at[2, pl.ds(0, 2)], load_sem.at[7]),
        pltpu.make_async_copy(field.at[pl.ds(0, 2)], rim.at[2, pl.ds(2, 2)], load_sem.at[8]),
    ]
    field_loads = [
        pltpu.make_async_copy(field.at[pl.ds(16 * n, 16)], x3.at[1, pl.ds(2 + 16 * n, 16)], field_sem.at[n])
        for n in range(4)
    ]
    kernel_loads = [
        pltpu.make_async_copy(
            src, wmat.at[conv, pl.ds(q, 3), :, :, pl.ds(q * C, C)], load_sem.at[1 + 2 * conv + q]
        )
        for conv, src in enumerate((k_one, k_two)) for q in range(2)
    ]
    bias_loads = [
        pltpu.make_async_copy(src, bias.at[conv], load_sem.at[9 + conv]) for conv, src in enumerate((b_one, b_two))
    ]
    early = field_loads[:1] + kernel_loads[:2] + bias_loads[:1]

    def start(copies):
        for c in copies:
            c.start()

    pl.when(me_blk == blks - 1)(lambda: start(small_loads + early))
    pl.when(me_blk < blks - 1)(lambda: start(early + small_loads))
    start(field_loads[1:] + kernel_loads[2:] + bias_loads[1:])

    for conv in range(2):
        wmat[conv, 0, :, :, C:] = jnp.zeros((3, C, C), BF16)
        wmat[conv, 3, :, :, :C] = jnp.zeros((3, C, C), BF16)
    for t in range(3):
        x3[t, X_ZERO] = jnp.zeros((SIDE, C), BF16)
        h3[0, t, H_ZERO] = jnp.zeros((SIDE, C), BF16)
        h3[1, t, H_ZERO] = jnp.zeros((SIDE, C), BF16)
    wown[...] = jnp.zeros(wown.shape, F32)

    def start_of(row, device):
        return jnp.minimum(lax.rem(row - device * SIDE + RIM + 2 * n_total, n_total), 2 * RIM) - RIM

    row_i = lax.broadcasted_iota(I32, (SIDE, SIDE), 0)
    col_i = lax.broadcasted_iota(I32, (SIDE, SIDE), 1)

    def prepare(to):
        for slot in range(SLOTS):
            wown[slot, 64:128] = jnp.where(slot < live_s[0], wts[slot], 0).astype(F32)
        for n, flag in enumerate((last, first)):
            turn = jnp.where(flag == 1, SIDE - 1 - col_i, col_i)
            turn = jnp.where(row_i == turn, 1.0, 0.0).astype(BF16)
            pair = jnp.concatenate([rim[2, 2 * n], rim[2, 2 * n + 1]], axis=-1)
            pair = jnp.dot(turn, pair, preferred_element_type=F32).astype(BF16)
            for i in range(2):
                rim[to, 2 * n + i] = pair[:, i * C : i * C + C]
            row = (128, 32)[n]
            line = (126, 64)[n]
            mine = jnp.concatenate(
                [sum(wown[p, pl.ds(row - start_of(rows_s[p, 0], me), RIM)] for p in range(SLOTS))]
                + [wown[p, line : line + 2] for p in range(SLOTS)] + [jnp.zeros((2, SIDE), F32)], axis=0)
            w_send[to, n] = jnp.dot(mine.astype(BF16), turn, preferred_element_type=F32)

    def exchange(n, at):
        return [
            pltpu.make_async_remote_copy(
                src_ref=src, dst_ref=dst, send_sem=send_sem.at[n, m], recv_sem=recv_sem.at[n, m],
                device_id=(after, before)[n], device_id_type=MESH,
            )
            for m, (src, dst) in enumerate((
                (rim.at[at, pl.ds(2 * n, 2)], rim_in.at[n]),
                (w_send.at[at, n], w_in.at[n]),
                (rows, rows_in.at[n]),
            ))
        ]

    exchanges = [exchange(n, 0) for n in range(2)]

    def send(at):
        pl.semaphore_wait(barrier, 2)
        for n in range(2):
            for c in exchange(n, at):
                c.start()

    def shift_field(start, count):
        left, _, right = shifts(x3[1, start : start + count].astype(F32))
        x3[0, start : start + count] = left.astype(BF16)
        x3[2, start : start + count] = right.astype(BF16)

    def stage(body):
        pl.when(me >= 0)(body)

    def run_parts(src, first_row, pairs, mirrored):
        return [
            tuple(pair_rows(src[2 - t if mirrored else t, pl.ds(first_row + 2 * p, 2 * pairs)]) for p in range(2))
            for t in range(3)
        ]


    def hidden_of(acc):
        h = unpair(acc)
        h = silu(h.reshape(-1, SIDE, C) + bias[0].reshape(1, 1, C))
        return [v.astype(BF16) for v in shifts(h)]

    def first_conv(view, first_row, pairs, mirrored):
        made = hidden_of(pair_dot(run_parts(x3, first_row, pairs, mirrored), wmat, 0))
        for t in range(3):
            h3[view, t, pl.ds(first_row, 2 * pairs)] = made[t]

    def second_conv(view, pair, pairs, mirrored):
        acc = pair_dot(run_parts(h3.at[view], 2 * pair, pairs, mirrored), wmat, 1)
        r = unpair(acc).reshape(2 * pairs, SIDE, C) + bias[1].reshape(1, 1, C)
        r = r + x3[1, pl.ds(2 + 2 * pair, 2 * pairs)].astype(F32)
        r_all[view, pl.ds(2 * pair, 2 * pairs)] = r
        if view == 0:
            base[pl.ds(2 * pair, 2 * pairs)] = r.astype(BF16)

    @pl.when(me_blk == blks - 1)
    def _():
        for c in small_loads:
            c.wait()
        prepare(0)
        send(0)

    field_loads[0].wait()
    shift_field(2, 16)
    for c in kernel_loads[:2] + bias_loads[:1]:
        c.wait()
    first_conv(0, 2, 7, False)

    @pl.when(me_blk < blks - 1)
    def _():
        for c in small_loads:
            c.wait()

    for c in field_loads[1:]:
        c.wait()

    @stage
    def _():
        shift_field(18, 48)
        first_conv(0, 16, 8, False)
        prepare(1)

    pl.when(jnp.logical_and(me_blk > 0, me_blk < blks - 1))(lambda: send(1))

    @stage
    def _():
        first_conv(0, 32, 8, False)
        first_conv(0, 48, 8, False)

    for c in kernel_loads[2:] + bias_loads[1:]:
        c.wait()

    @stage
    def _():
        second_conv(0, 1, 8, False)
        second_conv(0, 9, 8, False)
        second_conv(0, 17, 8, False)
        second_conv(0, 25, 6, False)

    writes = []
    for n, flag in enumerate((first, last)):
        bulk = pl.ds((2, RIM)[n], RIM - 2)
        writes.append(pltpu.make_async_copy(base.at[bulk], base_out.at[bulk], out_sem.at[2 + n]))
        pl.when(flag == 0)(writes[n].start)
    pl.when(jnp.logical_and(me_blk == 0, me > 0))(lambda: send(1))

    @pl.when(boundary)
    def _():
        b = jnp.where(me_blk == 0, 0, 15)
        first_conv(1, 2 * (1 + b), 8, True)
        first_conv(1, 2 * (9 + b), 8, True)

    @pl.when(boundary)
    def _():
        b = jnp.where(me_blk == 0, 0, 15)
        second_conv(1, 1 + b, 8, True)
        second_conv(1, 9 + b, 7, True)

    pl.when(me == 0)(lambda: send(1))

    own_starts = [start_of(rows_s[p, 0], me) for p in range(SLOTS)]

    def lanes(ref, r):
        return jnp.concatenate([ref(r[0]), ref(r[1])], axis=-1)

    def items_first(items):
        parts = [
            tuple(
                jnp.concatenate([
                    lanes(lambda i: x3[t + m * (2 - 2 * t), i], r[2 * p : 2 * p + 2]) for r, m in items
                ], axis=0)
                for p in range(2)
            )
            for t in range(3)
        ]
        return hidden_of(pair_dot(parts, wmat, 0))

    def items_second(items):
        parts = [
            tuple(
                jnp.concatenate([
                    lanes(lambda i: h3[v, t + m * (2 - 2 * t), i], r[2 * p : 2 * p + 2]) for v, r, m, _ in items
                ], axis=0)
                for p in range(2)
            )
            for t in range(3)
        ]
        r = unpair(pair_dot(parts, wmat, 1)) + bias[1].reshape(1, 1, 1, C)
        return [
            [r[n, q] + x3[1, residual[q]].astype(F32) for q in range(2)]
            for n, (_, _, _, residual) in enumerate(items)
        ]

    own_first, own_second, own_lead, own_weights = [], [], [], []
    for p in range(SLOTS):
        s = own_starts[p]
        e = s + SIDE - 1
        top = s > 0
        own_first.append((
            (jnp.where(top, X_ZERO, e + 1), jnp.where(top, s + 2, e + 2), jnp.where(top, s + 3, X_ZERO), X_ZERO), 0))
        own_second.append((
            0,
            (jnp.where(top, H_ZERO, e - 1), jnp.where(top, H_EDGE + p, e),
             jnp.where(top, s + 2, H_EDGE + p), jnp.where(top, s + 3, H_ZERO)),
            0,
            (jnp.where(top, s + 2, e + 1), jnp.where(top, s + 3, e + 2)),
        ))
        own_lead.append(jnp.where(top, s, e - 1))
        own_weights.append([jnp.where(top, wown[p, 64 + q : 65 + q], wown[p, 126 + q : 127 + q]) for q in range(2)])
    own_first.append(((X_ZERO, 2, 3, X_ZERO), 0))
    own_second.append((0, (H_ZERO, H_EDGE + 3, 2, 3), 0, (2, 3)))

    @stage
    def _():
        made = items_first(own_first)
        for t in range(3):
            for n in range(4):
                h3[0, t, H_EDGE + n] = made[t][2 * n]

    @stage
    def _():
        own_result = items_second(own_second)
        for n in range(4):
            for q in range(2):
                own_rows[2 * n + q] = own_result[n][q]

    cov[...] = sum(wown[p, pl.ds(64 - own_starts[p], SIDE)] for p in range(SLOTS))

    def own_at(where, row):
        return sum(
            jnp.where(jnp.logical_and(own_starts[p] == where, p < live_s[0]), wts[p, row : row + 1], 0)
            for p in range(SLOTS)
        ).astype(F32)

    def spread(columns, n):
        return jnp.broadcast_to(columns[:, n : n + 1], (SIDE, C))

    def in_range(row):
        return jnp.logical_and(row >= 0, row < SIDE)

    def coefficients(pairs):
        made = [
            jnp.where(in_range(row), w / cov[pl.ds(jnp.clip(row, 0, SIDE - 1), 1)], 0.0) for w, row in pairs
        ]
        made += [jnp.zeros((1, SIDE), F32)] * (-len(made) % 8)
        return jnp.concatenate(made, axis=0).T

    def settle(sides):
        items, tails, starts = [], [], {}
        for n in sides:
            flag = (first, last)[n]
            for c in exchanges[n]:
                c.wait_recv()
            rim_rows = slice((0, 66)[n], (2, 68)[n])
            left, _, right = shifts(rim_in[n].astype(F32))
            x3[1, rim_rows] = rim_in[n]
            x3[0, rim_rows] = left.astype(BF16)
            x3[2, rim_rows] = right.astype(BF16)
            starts[n] = [
                start_of(rows_in[n, p, 0], me - 1 if n == 0 else me + 1) + (-SIDE, SIDE)[n] for p in range(SLOTS)
            ]
            pair_first, pair_second = (0, 32)[n], (0, 31)[n]
            static = H_EDGE + 4 + n
            items += [
                (tuple(2 * pair_first + j for j in range(4)), 0),
                (tuple(2 * pair_first + j for j in range(4)), flag),
                ((X_ZERO, 1, 2, X_ZERO) if n == 0 else (65, 66, X_ZERO, X_ZERO), 0),
            ]
            four = tuple(2 * pair_second + j for j in range(4))
            tails += [
                (0, four, 0, (2 * pair_second + 2, 2 * pair_second + 3)),
                (flag, four, flag, (2 * pair_second + 2, 2 * pair_second + 3)),
                (0, (H_ZERO, static, 1, 2), 0, (1, 2)) if n == 0 else (0, (63, 64, static, H_ZERO), 0, (65, 66)),
            ]
            for p in range(SLOTS):
                at = H_EDGE + 6 + 3 * n + p
                if n == 0:
                    e = jnp.clip(starts[n][p] + SIDE - 1, 0, RIM - 1)
                    items.append(((e + 1, e + 2, X_ZERO, X_ZERO), flag))
                    tails.append((flag, (jnp.maximum(e - 1, 0), e, at, H_ZERO), flag, (e + 1, e + 2)))
                else:
                    s = jnp.clip(starts[n][p], RIM, SIDE - 1)
                    items.append(((X_ZERO, s + 2, s + 3, X_ZERO), flag))
                    tails.append((flag, (H_ZERO, at, s + 2, s + 3), flag, (s + 2, s + 3)))

        @stage
        def _():
            made = items_first(items)
            for k, n in enumerate(sides):
                flag, pair_first = (first, last)[n], (0, 32)[n]
                for t in range(3):
                    m = made[t][12 * k : 12 * k + 12]
                    h3[flag, t, 2 * pair_first : 2 * pair_first + 2] = m[2:4]
                    h3[0, t, 2 * pair_first : 2 * pair_first + 2] = m[0:2]
                    h3[0, t, H_EDGE + 4 + n] = m[4]
                    for p in range(SLOTS):
                        h3[flag, t, H_EDGE + 6 + 3 * n + p] = m[6 + 2 * p]

        @stage
        def _():
            result = items_second(tails)
            for k, n in enumerate(sides):
                finish(n, result[6 * k : 6 * k + 6], starts[n])

        for n in sides:
            bulk = pl.ds((2, RIM)[n], RIM - 2)
            late = pltpu.make_async_copy(blend.at[bulk], base_out.at[bulk], out_sem.at[2 + n])
            pl.when((first, last)[n] == 1)(late.start)

    def finish(n, result, starts):
        flag, half, row = (first, last)[n], (0, RIM)[n], (0, SIDE - 2)[n]
        for view, i in ((flag, 1), (0, 0)):
            for q in range(2):
                r_all[view, row + q] = result[i][q]

        near = w_in[n, 0:RIM]
        cover = cov[half : half + RIM] + near
        cov[half : half + RIM] = cover

        pairs, indices = [], [None] * N_ROWS
        for p in range(SLOTS):
            lead = starts[p] + SIDE - 2 if n == 0 else starts[p]
            for q in range(2):
                k = 2 * p + q
                pairs.append((w_in[n, RIM + k : RIM + k + 1], lead + q))
                indices[6 + 6 * n + k] = jnp.where(in_range(lead + q), lead + q, RIM - 2 + 2 * n + q)
        if n == 0:
            pairs += [(own_at(-1, 1), 0), (own_at(0, 0), 0), (own_at(0, 1), 1)]
            for p in range(SLOTS):
                for q in range(2):
                    pairs.append((own_weights[p][q], own_lead[p] + q))
                    indices[2 * p + q] = own_lead[p] + q
        else:
            pairs.append((own_at(1, SIDE - 2), SIDE - 1))
        columns = coefficients(pairs)
        for k in range(6):
            at = 6 + 6 * n + k
            edge[at] = ((result[3 + k // 2][k % 2] - r_all[flag, indices[at]]) * spread(columns, k)).astype(BF16)
        if n == 0:
            for k in range(6):
                edge[k] = ((own_rows[k] - r_all[0, indices[k]]) * spread(columns, 9 + k)).astype(BF16)
        lane = lax.broadcasted_iota(I32, (8, C), 1)
        packed = index[...] if n == 0 else jnp.zeros((8, C), I32)
        for k in range(N_ROWS):
            if indices[k] is not None:
                packed = jnp.where(lane == k, indices[k], packed)
        index[...] = packed

        share = (near / cover).T
        for r in range(half, half + RIM):
            v = r_all[0, r]
            mixed = v + (r_all[1, r] - v) * spread(share, r - half)
            if row <= r < row + 2:
                base[r] = jnp.where(flag == 1, mixed, v).astype(BF16)
            else:
                blend[r] = mixed.astype(BF16)

        def plus(r, v):
            base[r] = (base[r].astype(F32) + v).astype(BF16)

        if n == 0:
            plus(0, (result[2][1] - result[0][0]) * spread(columns, 6)
                 + (own_rows[6] - result[0][0]) * spread(columns, 7))
            plus(1, (own_rows[7] - result[0][1]) * spread(columns, 8))
        else:
            plus(SIDE - 1, (result[2][0] - result[0][1]) * spread(columns, 6))

    @pl.when(me <= 1)
    def _():
        settle((1,))
        settle((0,))

    @pl.when(me > 1)
    def _():
        settle((1, 0))

    tail = [
        pltpu.make_async_copy(edge, edge_out, out_sem.at[0]),
        pltpu.make_async_copy(index, index_out, out_sem.at[1]),
        pltpu.make_async_copy(base.at[pl.ds(0, 2)], base_out.at[pl.ds(0, 2)], out_sem.at[4]),
        pltpu.make_async_copy(base.at[pl.ds(SIDE - 2, 2)], base_out.at[pl.ds(SIDE - 2, 2)], out_sem.at[5]),
    ]
    for c in tail:
        c.start()
    writes += tail
    for n in range(2):
        for c in exchanges[n]:
            c.wait_send()
    for c in writes:
        c.wait()


def place(index, base, edge, out, index_s, base_v, edge_v, load_sem, out_sem):
    loads = [
        pltpu.make_async_copy(index, index_s, load_sem.at[0]),
        pltpu.make_async_copy(edge, edge_v, load_sem.at[1]),
    ] + [
        pltpu.make_async_copy(base.at[pl.ds(16 * n, 16)], base_v.at[pl.ds(16 * n, 16)], load_sem.at[2 + n])
        for n in range(4)
    ]
    for c in loads:
        c.start()
    for c in loads:
        c.wait()
    rows = [index_s[0, n] for n in range(N_ROWS)]
    for n in range(0, N_ROWS, 2):
        v = [(base_v[rows[n + q]].astype(F32) + edge_v[n + q].astype(F32)).astype(BF16) for q in range(2)]
        for q in range(2):
            base_v[rows[n + q]] = v[q]
    stores = [
        pltpu.make_async_copy(base_v.at[pl.ds(16 * n, 16)], out.at[pl.ds(16 * n, 16)], out_sem.at[n]) for n in range(4)
    ]
    for c in stores:
        c.start()
    for c in stores:
        c.wait()


def shards(field, patch_rows, flips, blend_weights, live, kernel_one, bias_one, kernel_two, bias_two):
    faces, blks = lax.axis_size("face"), lax.axis_size("blk")
    anywhere = pl.BlockSpec(memory_space=pl.ANY)
    base, edge, index = pl.pallas_call(
        functools.partial(work, faces, blks),
        out_shape=(
            jax.ShapeDtypeStruct((SIDE, SIDE, C), BF16),
            jax.ShapeDtypeStruct((N_ROWS, SIDE, C), BF16),
            jax.ShapeDtypeStruct((8, C), I32),
        ),
        in_specs=[anywhere] * 8,
        out_specs=(anywhere,) * 3,
        scratch_shapes=[
            pltpu.VMEM((3, X_ZERO + 1, SIDE, C), BF16),
            pltpu.VMEM((2, 3, H_EDGE + N_EDGE, SIDE, C), BF16),
            pltpu.VMEM((2, SIDE, SIDE, C), F32),
            pltpu.VMEM((2, 4, 3, C, 2 * C), BF16),
            pltpu.VMEM((SLOTS, SIDE, SIDE), I32),
            pltpu.VMEM((2, 2, 40, SIDE), F32),
            pltpu.VMEM((2, 40, SIDE), F32),
            pltpu.VMEM((3, 4, SIDE, C), BF16),
            pltpu.VMEM((2, 2, SIDE, C), BF16),
            pltpu.VMEM((2, SLOTS, SIDE), I32),
            pltpu.VMEM((SLOTS, 192, SIDE), F32),
            pltpu.VMEM((SIDE, SIDE), F32),
            pltpu.VMEM((SIDE, SIDE, C), BF16),
            pltpu.VMEM((SIDE, SIDE, C), BF16),
            pltpu.VMEM((8, SIDE, C), F32),
            pltpu.VMEM((N_ROWS, SIDE, C), BF16),
            pltpu.VMEM((8, C), I32),
            pltpu.VMEM((2, 1, C), F32),
            pltpu.SMEM((SLOTS, SIDE), I32),
            pltpu.SMEM((1,), I32),
            pltpu.SemaphoreType.DMA((4,)),
            pltpu.SemaphoreType.DMA((11,)),
            pltpu.SemaphoreType.DMA((2, 3)),
            pltpu.SemaphoreType.DMA((2, 3)),
            pltpu.SemaphoreType.DMA((6,)),
        ],
        compiler_params=pltpu.CompilerParams(
            collective_id=0, has_side_effects=True, vmem_limit_bytes=62 * 2**20
        ),
    )(
        field, patch_rows, live, blend_weights, kernel_one, kernel_two,
        bias_one.reshape(1, C), bias_two.reshape(1, C),
    )
    return pl.pallas_call(
        place,
        out_shape=jax.ShapeDtypeStruct((SIDE, SIDE, C), BF16),
        in_specs=[anywhere] * 3,
        out_specs=anywhere,
        scratch_shapes=[
            pltpu.SMEM((8, C), I32),
            pltpu.VMEM((SIDE, SIDE, C), BF16),
            pltpu.VMEM((N_ROWS, SIDE, C), BF16),
            pltpu.SemaphoreType.DMA((6,)),
            pltpu.SemaphoreType.DMA((4,)),
        ],
        compiler_params=pltpu.CompilerParams(vmem_limit_bytes=62 * 2**20),
    )(index, base, edge)


def solution(mesh):
    split = ("face", "blk")
    placed = (P(split, None, None), P(split, None), P(split, None), P(split, None, None), P(split), P(), P(), P(), P())
    return jax.shard_map(shards, mesh=mesh, in_specs=placed, out_specs=P(split, None, None), check_vma=False)
```
